512 devices in a mesh: lat: 32 (over z_lo, x), lon: 16 (over y, z_hi, core).
Axes of the slice: x: 4, y: 4, z: 16 (z_hi: 2, z_lo: 8; z = z_hi * 8 + z_lo), core: 2. Of those that a mesh axis runs over, the one named last changes fastest.
Arguments:
- grid_field: bfloat16 [512, 2880, 64], P('lat', 'lon'), may hold values from -6 to 6
- disco_reach: int32 [512], P('lat'), may hold values from 1 to 20, as said below
- disco_taps: float32 [512, 492], P('lat'), may hold values from -1 to 1
- disco_weight: bfloat16 [4, 64, 64], replicated, may hold values from -0.375 to 0.375
- legendre: bfloat16 [512, 32, 768], P('lat', 'lon'), may hold values from -0.25 to 0.25
- spectral_mixing_weight: bfloat16 [768, 2, 64, 64], P('lat'), may hold values from -0.5 to 0.5
Outputs:
- block_out: bfloat16 [512, 2880, 64], P('lat', 'lon')
The draws below stay inside these ranges and needn't reach their ends.
Inputs may be any that keep to these rules, and one draw needn't show every extreme that they name: `disco_reach`: the rows at both poles reach 20.
All inputs are finite; a program needn't handle non-finite values.
Results may differ from the reference program's by a relative error of at most 0.02.
Values may be sent and summed in bfloat16 or wider, within the bound.
No kernel may reach another device: no remote copies, remote signals or barrier semaphores. Data moves between devices by JAX's collectives and lax.ppermute only.
A program may use at most 128 MiB of HBM per device.

```python
import math
import jax
import jax.numpy as jnp
from jax import lax

CH = 64
NLON = 2880
LDEG = 768
HMAX = 20
BASES = 4
NLAT = 512
MODES = 32


def draw_disco_reach(key, part):
    rows = jnp.arange(NLAT, dtype=jnp.int32)
    distance = jnp.abs(2 * rows + 1 - NLAT)
    span = NLAT - 1
    baseline = 1 + (HMAX - 1) * distance * distance // (span * span)
    jitter = jax.random.randint(key, (NLAT,), 0, 2, dtype=jnp.int32)
    return jnp.minimum(baseline + jitter, HMAX).astype(jnp.int32)


def steps_of(stream_key, shape, split, smallest, largest):
    gain = 1.0
    for position, blocks in split:
        draws = jax.random.uniform(jax.random.fold_in(jax.random.fold_in(stream_key, 6), position), (blocks,), jnp.float32, smallest / len(split), largest / len(split))
        gain = gain * jnp.repeat(jnp.exp(draws), shape[position] // blocks).reshape((-1,) + (1,) * (len(shape) - 1 - position))
    return gain


def bell_draw(rng, shape, scale, bound, shards=(), held_as=jnp.bfloat16):
    drawn = scale * jax.random.normal(rng, shape, jnp.float32)
    if shards:
        drawn = drawn * steps_of(rng, shape, shards, -0.22, 0.18)
    return jnp.clip(drawn, -bound, bound).astype(held_as)


def setup_inputs(seed: int = 0) -> dict:
    key_of = jax.random.split(jax.random.key(seed), 7)
    return {
        "grid_field": bell_draw(key_of[0], (NLAT, NLON, CH), 1.0, 6.0, ((0, 32), (1, 16))),
        "disco_reach": draw_disco_reach(jax.random.fold_in(key_of[6], 71), 0),
        "disco_taps": bell_draw(key_of[2], (NLAT, BASES * 3 * (2 * HMAX + 1)), 0.2, 1.0, ((0, 32),), jnp.float32),
        "disco_weight": bell_draw(key_of[3], (BASES, CH, CH), (BASES * CH) ** -0.5, 0.375),
        "legendre": bell_draw(key_of[4], (NLAT, MODES, LDEG), NLAT ** -0.5, 0.25, ((0, 32), (1, 16))),
        "spectral_mixing_weight": bell_draw(key_of[5], (LDEG, 2, CH, CH), (2 * CH) ** -0.5, 0.5, ((0, 32),)),
    }


row_group = 4

def angles(columns, orders):
    residues = columns[:, None] * orders[None, :] % NLON
    return residues.astype(jnp.float32) * (2.0 * math.pi / NLON)

def forward_table(columns, orders):
    phases = angles(columns, orders)
    factor = 1.0 / math.sqrt(NLON)
    return jnp.stack([jnp.cos(phases) * factor, -jnp.sin(phases) * factor], axis=1).astype(jnp.bfloat16)

def inverse_table(orders, columns, mode_count):
    phases = angles(columns, orders)
    factor = 1.0 / math.sqrt(mode_count)
    return jnp.stack([jnp.cos(phases).T * factor, -jnp.sin(phases).T * factor], axis=0).astype(jnp.bfloat16)

def reference(grid_field, disco_reach, disco_taps, disco_weight, legendre, spectral_mixing_weight):
    tap_count = 2 * HMAX + 1
    wrapped = jnp.concatenate([grid_field[:, NLON - HMAX:], grid_field, grid_field[:, :HMAX]], axis=1)
    zero_row = jnp.zeros((1, NLON + 2 * HMAX, CH), grid_field.dtype)
    extended = jnp.concatenate([zero_row, wrapped, zero_row], axis=0).reshape(NLAT + 2, (NLON + 2 * HMAX) * CH)
    offsets = jnp.abs(jnp.arange(tap_count, dtype=jnp.int32) - HMAX)
    within = offsets[None, :] <= disco_reach[:, None]
    kernel_coef = jnp.where(within[:, None, None, :], disco_taps.reshape(NLAT, BASES, 3, tap_count), 0.0)
    kernel_coef = kernel_coef.reshape(NLAT, BASES, 3 * tap_count)
    firsts = jnp.arange(NLAT // row_group, dtype=jnp.int32) * row_group
    forward_pass = forward_table(jnp.arange(NLON, dtype=jnp.int32), jnp.arange(MODES, dtype=jnp.int32)).astype(jnp.float32)

    def spectra_block(first):
        row_portion_slice = lax.dynamic_slice_in_dim(grid_field, first, row_group, 0).astype(jnp.float32)
        final_output = jnp.einsum('blv,lis->bsiv', row_portion_slice, forward_pass)
        return final_output.reshape(row_group, MODES, 2 * CH).astype(jnp.bfloat16)
    spectra = lax.map(spectra_block, firsts).reshape(NLAT, MODES, 2 * CH)
    degrees = jnp.arange(LDEG, dtype=jnp.int32)
    orders = jnp.arange(MODES, dtype=jnp.int32)
    leg_masked = jnp.where((degrees[None, :] >= orders[:, None])[None], legendre, jnp.zeros((), legendre.dtype))
    leg_wide = leg_masked.astype(jnp.float32)
    coeffs = jnp.einsum('iml,imc->lmc', leg_wide, spectra.astype(jnp.float32))
    coeffs_low = coeffs.astype(jnp.bfloat16)
    real_part = spectral_mixing_weight[:, 0]
    imag_part = spectral_mixing_weight[:, 1]
    upper = jnp.concatenate([real_part, imag_part], axis=2)
    lower = jnp.concatenate([-imag_part, real_part], axis=2)
    complex_block = jnp.concatenate([upper, lower], axis=1)
    mixed_modes = jnp.einsum('lmc,lcd->lmd', coeffs_low.astype(jnp.float32), complex_block.astype(jnp.float32)).astype(jnp.bfloat16)
    grid_modes = jnp.einsum('iml,lmc->imc', leg_wide, mixed_modes.astype(jnp.float32)).astype(jnp.bfloat16)
    back = inverse_table(orders, jnp.arange(NLON, dtype=jnp.int32), MODES).astype(jnp.float32)
    weight_wide = disco_weight.astype(jnp.float32)

    def result_output_block(first):
        slab = lax.dynamic_slice_in_dim(extended, first, row_group + 2, 0)
        windows = jnp.stack([slab[a:a + row_group, s * CH:(s + NLON) * CH] for a in range(3) for s in range(tap_count)], axis=1).astype(jnp.float32)
        portion = lax.dynamic_slice_in_dim(kernel_coef, first, row_group, 0).astype(jnp.float32)
        basis_sums = jnp.einsum('rkt,rtx->rkx', portion, windows).astype(jnp.bfloat16)
        basis_sums = basis_sums.reshape(row_group, BASES, NLON, CH).astype(jnp.float32)
        disco_out = jnp.einsum('rkjc,kcd->rjd', basis_sums, weight_wide)
        modes_part = lax.dynamic_slice_in_dim(grid_modes, first, row_group, 0).astype(jnp.float32)
        spectral_out = jnp.einsum('impc,pmj->ijc', modes_part.reshape(row_group, MODES, 2, CH), back).astype(jnp.bfloat16)
        row_portion_slice = lax.dynamic_slice_in_dim(grid_field, first, row_group, 0).astype(jnp.float32)
        mixed = spectral_out.astype(jnp.float32) + disco_out
        return (row_portion_slice + jax.nn.gelu(mixed, approximate=True)).astype(jnp.bfloat16)
    return lax.map(result_output_block, firsts).reshape(NLAT, NLON, CH)
```

```python
import math

import jax
import jax.numpy as jnp
import numpy as np
from jax import lax
from jax.experimental import pallas as pl
from jax.experimental.pallas import tpu as pltpu
from jax.sharding import Mesh
from jax.sharding import PartitionSpec as P

NLON = 2880
MODES = 32
HMAX = 20
TAPS = 2 * HMAX + 1
BASES = 4
LANES = 128
BF16 = jnp.bfloat16
F32 = jnp.float32
PLANE = ("x", "y", "core")
LINE = ("zh", "zl")
ORDER_GROUP = ("y", "core")


def orders_by_group():
    out = np.zeros((8, 4), np.int64)
    for y in range(4):
        for core in range(2):
            for zh in range(2):
                for odd in range(2):
                    out[y * 2 + core, zh * 2 + odd] = (y * 4 + zh * 2 + core) * 2 + odd
    return out.reshape(-1)


def tables(lon_cols):
    residues = (orders_by_group()[:, None] * np.arange(NLON)[None, :]) % NLON
    phases = residues.astype(np.float32) * np.float32(2.0 * math.pi / NLON)
    waves = np.stack([np.cos(phases), -np.sin(phases)], axis=1).astype(np.float32)
    waves = waves.reshape(MODES, 2, NLON // lon_cols, lon_cols).transpose(2, 0, 1, 3)
    forward = (waves * np.float32(1.0 / math.sqrt(NLON))).astype(BF16)
    inverse = (waves * np.float32(1.0 / math.sqrt(MODES))).astype(BF16)
    return forward, inverse


def toeplitz_kernel(ext_ref, base_ref, weight_ref, out_ref, band_ref):
    row = pl.program_id(0)

    @pl.when(row == 0)
    def _():
        band_ref[...] = jnp.zeros_like(band_ref)

    r = lax.broadcasted_iota(jnp.int32, (LANES, LANES), 0)
    s = lax.broadcasted_iota(jnp.int32, (LANES, LANES), 1)
    for a in range(3):
        for k in range(BASES):
            line = jnp.broadcast_to(base_ref[0, k * 3 + a][None, :], (LANES, LANES))
            circ = pltpu.roll(line, 0, 1, stride=1, stride_axis=0)
            near = jnp.where(s <= r, circ, 0.0).astype(BF16)
            far = jnp.where(s > r, circ, 0.0)[:48].astype(BF16)
            band_ref[a * 256 : a * 256 + LANES, k * LANES : (k + 1) * LANES] = near
            band_ref[a * 256 + LANES : a * 256 + LANES + 48, k * LANES : (k + 1) * LANES] = far
    rows = [ext_ref[row + a] for a in range(3)]
    zeros = jnp.zeros((64, LANES), BF16)
    upper = jnp.concatenate(rows, axis=1)
    lower = jnp.concatenate([p for v in rows for p in (v[:, LANES:], zeros)], axis=1)
    sums = jnp.dot(
        jnp.concatenate([upper, lower], axis=0), band_ref[...], preferred_element_type=F32
    ).astype(BF16)
    stacked = jnp.concatenate(
        [
            jnp.concatenate(
                [sums[u * 64 : (u + 1) * 64, k * LANES : (k + 1) * LANES] for u in range(2)], axis=1
            )
            for k in range(BASES)
        ],
        axis=0,
    )
    mixed = jnp.dot(weight_ref[...], stacked, preferred_element_type=F32)
    out_ref[0] = mixed[:, : out_ref.shape[2]]


def disco(field, disco_reach, disco_taps, disco_weight):
    lat_rows, channels, lon_cols = field.shape
    core = lax.axis_index("core")
    even_row = lax.axis_index("x") % 2 == 0
    head, tail = field[:, :, :HMAX], field[:, :, lon_cols - HMAX :]
    lon = ("y", "zh", "core")
    near_pairs = [(i, i ^ 1) for i in range(16)]
    far_pairs = [(i, (i + 1) % 16 if i % 2 else (i - 1) % 16) for i in range(16)]
    near = lax.ppermute(jnp.where(core == 0, tail, head), lon, near_pairs)
    far = lax.ppermute(jnp.where(core == 0, head, tail), lon, far_pairs)
    left = jnp.where(core == 0, far, near)
    right = jnp.where(core == 0, near, far)
    blank = jnp.zeros((lat_rows, channels, 256 - lon_cols - 2 * HMAX), BF16)
    wide = jnp.concatenate([left, field, right, blank], axis=2)
    lat = ("zl", "x")
    even_pairs = [(i, i ^ 1) for i in range(32)]
    odd_pairs = [(i, i + 1 if i % 2 else i - 1) for i in range(1, 31)]
    first, last = wide[:1], wide[lat_rows - 1 :]
    one = lax.ppermute(jnp.where(even_row, last, first), lat, even_pairs)
    two = lax.ppermute(jnp.where(even_row, first, last), lat, odd_pairs)
    extended = jnp.concatenate(
        [jnp.where(even_row, two, one), wide, jnp.where(even_row, one, two)], axis=0
    )
    offsets = jnp.abs(jnp.arange(TAPS, dtype=jnp.int32) - HMAX)
    within = offsets[None, :] <= disco_reach[:, None]
    coef = jnp.where(
        within[:, None, :], disco_taps.reshape(lat_rows, BASES * 3, TAPS), 0.0
    )
    base = jnp.concatenate(
        [
            coef[:, :, :1],
            jnp.zeros((lat_rows, BASES * 3, LANES - TAPS), F32),
            coef[:, :, :0:-1],
        ],
        axis=2,
    )
    weight = disco_weight.transpose(2, 0, 1).reshape(channels, BASES * channels)
    return pl.pallas_call(
        toeplitz_kernel,
        grid=(lat_rows,),
        in_specs=[
            pl.BlockSpec(extended.shape, lambda i: (0, 0, 0)),
            pl.BlockSpec((1, BASES * 3, LANES), lambda i: (i, 0, 0)),
            pl.BlockSpec(weight.shape, lambda i: (0, 0)),
        ],
        out_specs=pl.BlockSpec((1, channels, lon_cols), lambda i: (i, 0, 0)),
        out_shape=jax.ShapeDtypeStruct((lat_rows, channels, lon_cols), F32),
        scratch_shapes=[pltpu.VMEM((768, BASES * LANES), BF16)],
        cost_estimate=pl.CostEstimate(
            flops=2 * lat_rows * 128 * 768 * 512, bytes_accessed=2**21, transcendentals=0
        ),
    )(extended, base, weight)


def exchange(cells, axes):
    return lax.all_to_all(cells, axes, split_axis=0, concat_axis=0, tiled=True)


def per_device(grid_field, disco_reach, disco_taps, disco_weight, legendre, mixing):
    lat_rows, lon_cols, channels = grid_field.shape
    wide = 2 * channels
    lon_place = lax.axis_index(("y", "zh", "core"))
    forward, inverse = tables(lon_cols)
    forward = lax.dynamic_index_in_dim(jnp.asarray(forward), lon_place, 0, keepdims=False)
    inverse = lax.dynamic_index_in_dim(jnp.asarray(inverse), lon_place, 0, keepdims=False)

    degrees = jnp.arange(legendre.shape[2], dtype=jnp.int32)
    orders = lon_place * 2 + jnp.arange(2, dtype=jnp.int32)
    masked = jnp.where(degrees[None, None, :] >= orders[None, :, None], legendre, jnp.zeros((), BF16))
    own = mixing.shape[0]
    masked = masked.reshape(lat_rows, 2, 8, 4, own).transpose(3, 1, 0, 2, 4)
    masked = masked.reshape(4, 1, 2, lat_rows, 8 * own)
    masked = jnp.broadcast_to(masked, (4, 2, 2, lat_rows, 8 * own)).reshape(8, 2, lat_rows, 8 * own)
    leg = exchange(masked, ("x", "zh")).reshape(4, 4, lat_rows, 8 * own)

    waves = jnp.einsum(
        "ijc,gqpj->gqipc",
        grid_field,
        forward.reshape(8, 4, 2, lon_cols),
        preferred_element_type=F32,
    ).astype(BF16)
    waves = waves.reshape(1, 8, 4 * lat_rows, wide)
    waves = jnp.broadcast_to(waves, (4, 8, 4 * lat_rows, wide)).reshape(32, 4 * lat_rows, wide)
    waves = exchange(waves, PLANE).reshape(4, 8, 4, lat_rows, wide)
    spectra = waves.astype(F32).sum(axis=1).astype(BF16)
    coeffs = jnp.einsum("xqil,xqiv->qlv", leg, spectra, preferred_element_type=F32).astype(BF16)
    coeffs = coeffs.reshape(2, 2, 8, own, wide).transpose(0, 2, 1, 3, 4).reshape(16, 2 * own, wide)
    coeffs = exchange(coeffs, LINE).astype(F32).sum(axis=0).astype(BF16).reshape(2, own, wide)
    real, imag = mixing[:, 0], mixing[:, 1]
    block = jnp.concatenate(
        [jnp.concatenate([real, imag], axis=2), jnp.concatenate([-imag, real], axis=2)], axis=1
    )
    mixed = jnp.einsum("qlv,lvw->qlw", coeffs, block, preferred_element_type=F32).astype(BF16)
    mixed = jnp.broadcast_to(mixed.reshape(1, 2 * own, wide), (16, 2 * own, wide))
    mixed = exchange(mixed, LINE).reshape(2, 8, 2, own, wide).transpose(0, 2, 1, 3, 4)
    mixed = mixed.reshape(4, 8 * own, wide)
    modes = jnp.einsum("xqil,qlv->xqiv", leg, mixed, preferred_element_type=F32).astype(BF16)
    modes = modes.reshape(4, 1, 4 * lat_rows, wide)
    modes = jnp.broadcast_to(modes, (4, 8, 4 * lat_rows, wide)).reshape(32, 4 * lat_rows, wide)
    modes = exchange(modes, PLANE).reshape(4, 8, 4, lat_rows, 2, channels)
    modes = modes.astype(F32).sum(axis=0).astype(BF16)
    spectral_out = jnp.einsum(
        "gqipc,gqpj->icj",
        modes,
        inverse.reshape(8, 4, 2, lon_cols),
        preferred_element_type=F32,
    ).astype(BF16)
    field = grid_field.transpose(0, 2, 1)
    disco_out = disco(field, disco_reach, disco_taps, disco_weight)
    combined = spectral_out.astype(F32) + disco_out
    out = (field.astype(F32) + jax.nn.gelu(combined, approximate=True)).astype(BF16)
    return out.transpose(0, 2, 1)


def solution(mesh):
    fine = Mesh(mesh.devices.reshape(8, 4, 4, 2, 2), ("zl", "x", "y", "zh", "core"))
    lat, lon = ("zl", "x"), ("y", "zh", "core")
    in_specs = (
        P(lat, lon, None),
        P(lat),
        P(lat, None),
        P(),
        P(lat, lon, None),
        P(lat, None, None, None),
    )
    return jax.shard_map(
        per_device, mesh=fine, in_specs=in_specs, out_specs=P(lat, lon, None), check_vma=False
    )
```

```python
import math

import jax
import jax.numpy as jnp
import numpy as np
from jax import lax
from jax.experimental import pallas as pl
from jax.experimental.pallas import tpu as pltpu
from jax.sharding import Mesh
from jax.sharding import PartitionSpec as P

NLON = 2880
MODES = 32
HMAX = 20
TAPS = 2 * HMAX + 1
BASES = 4
LANES = 128
BF16 = jnp.bfloat16
F32 = jnp.float32
LON = ("y", "zh", "core")


def table(lon_cols, scale):
    residues = (np.arange(MODES)[:, None] * np.arange(NLON)[None, :]) % NLON
    phases = residues.astype(np.float32) * np.float32(2.0 * math.pi / NLON)
    waves = np.stack([np.cos(phases), -np.sin(phases)], axis=0).astype(np.float32)
    waves = waves.reshape(2 * MODES, NLON // lon_cols, lon_cols).transpose(1, 0, 2)
    return (waves * np.float32(scale)).astype(BF16)


def first_half(shape):
    return lax.broadcasted_iota(jnp.int32, shape, len(shape) - 1) < 64


def forward_kernel(field_ref, table_ref, out_ref, rows_ref):
    rows = field_ref.shape[0]
    field = field_ref[...].reshape(rows * 64, field_ref.shape[2])
    waves = lax.dot_general(
        table_ref[...], field, (((1,), (1,)), ((), ())), preferred_element_type=F32
    )
    half = first_half((MODES, LANES))
    for m in range(rows // 2):
        re = waves[:MODES, m * LANES : (m + 1) * LANES]
        im = waves[MODES:, m * LANES : (m + 1) * LANES]
        rows_ref[pl.ds(2 * m, MODES, stride=rows), :] = jnp.where(half, re, pltpu.roll(im, 64, 1))
        rows_ref[pl.ds(2 * m + 1, MODES, stride=rows), :] = jnp.where(
            half, pltpu.roll(re, 64, 1), im
        )
    out_ref[...] = rows_ref[...].astype(BF16).reshape(out_ref.shape)


def spectra_kernel(waves_ref, leg_ref, out_ref):
    total = waves_ref[0].astype(F32)
    for n in range(1, waves_ref.shape[0]):
        total += waves_ref[n].astype(F32)
    spectra = total.astype(BF16)
    for x in range(4):
        out_ref[x, :, :LANES] = spectra
        out_ref[x, :, LANES:] = leg_ref[x]


def analysis_kernel(got_ref, coeff_ref, leg_ref):
    parts = []
    for q in range(2):
        pieces = [got_ref[x, q * 16 : (q + 1) * 16, :] for x in range(4)]
        both = jnp.concatenate(pieces, axis=0)
        leg_ref[q] = both[:, LANES:]
        parts.append(
            lax.dot_general(
                both[:, LANES:],
                both[:, :LANES],
                (((0,), (0,)), ((), ())),
                preferred_element_type=F32,
            )
        )
    for n in range(8):
        rows = jnp.concatenate([p[n * 24 : (n + 1) * 24] for p in parts], axis=0)
        coeff_ref[n] = rows.astype(BF16)


def mixing_kernel(coeff_ref, weight_ref, out_ref):
    total = coeff_ref[0].astype(F32)
    for n in range(1, coeff_ref.shape[0]):
        total += coeff_ref[n].astype(F32)
    lhs = jnp.concatenate([total[:, :64], total[:, 64:]], axis=0).astype(BF16)
    degree = lax.broadcasted_iota(jnp.int32, (96, LANES), 0) % 24
    acc = jnp.zeros((96, LANES), F32)
    for l in range(24):
        acc = jnp.where(
            degree == l, jnp.dot(lhs, weight_ref[l], preferred_element_type=F32), acc
        )
    turned = pltpu.roll(acc[48:], 64, 1)
    mixed = acc[:48] + jnp.where(first_half((48, LANES)), -turned, turned)
    mixed = mixed.astype(BF16)
    for n in range(out_ref.shape[0]):
        out_ref[n] = mixed


def synthesis_kernel(mixed_ref, leg_ref, out_ref):
    blocks = [mixed_ref[n].astype(F32) for n in range(8)]
    for q in range(2):
        mixed = jnp.concatenate([v[q * 24 : (q + 1) * 24] for v in blocks], axis=0)
        modes = jnp.dot(
            leg_ref[q][:, :192], mixed.astype(BF16), preferred_element_type=F32
        ).astype(BF16)
        for x in range(4):
            out_ref[x, q * 16 : (q + 1) * 16, :] = modes[x * 16 : (x + 1) * 16]


def modes_kernel(parts_ref, out_ref):
    total = parts_ref[0].astype(F32)
    for n in range(1, parts_ref.shape[0]):
        total += parts_ref[n].astype(F32)
    modes = total.astype(BF16)
    for n in range(out_ref.shape[0]):
        out_ref[n] = modes


def final_kernel(modes_ref, table_ref, disco_ref, field_ref, out_ref, rows_ref):
    rows, channels, cols = field_ref.shape
    for n in range(16):
        rows_ref[n * 32 : (n + 1) * 32, :] = modes_ref[n].astype(F32)
    half = first_half((MODES, LANES))
    for m in range(rows // 2):
        one = rows_ref[pl.ds(2 * m, MODES, stride=rows), :]
        two = rows_ref[pl.ds(2 * m + 1, MODES, stride=rows), :]
        re = jnp.where(half, one, pltpu.roll(two, 64, 1))
        im = jnp.where(half, pltpu.roll(one, 64, 1), two)
        spectral = lax.dot_general(
            jnp.concatenate([re, im], axis=0).astype(BF16),
            table_ref[...],
            (((0,), (0,)), ((), ())),
            preferred_element_type=F32,
        ).astype(BF16)
        for u in range(2):
            v = spectral[u * 64 : (u + 1) * 64].astype(F32) + disco_ref[2 * m + u]
            inner = math.sqrt(2.0 / math.pi) * (v + 0.044715 * (v * v * v))
            act = 0.5 * v * (1.0 + jnp.tanh(inner))
            out_ref[2 * m + u] = (field_ref[2 * m + u].astype(F32) + act).astype(BF16)


def call(kernel, out, *args, scratch=(), flops=10**7, smem=0):
    nbytes = sum(a.size * a.dtype.itemsize for a in args)
    vmem = pl.BlockSpec(memory_space=pltpu.VMEM)
    scalar = pl.BlockSpec(memory_space=pltpu.SMEM)
    return pl.pallas_call(
        kernel,
        out_shape=out,
        in_specs=[scalar] * smem + [vmem] * (len(args) - smem),
        out_specs=jax.tree.map(lambda _: vmem, out),
        scratch_shapes=scratch,
        compiler_params=pltpu.CompilerParams(vmem_limit_bytes=16 * 2**20),
        cost_estimate=pl.CostEstimate(flops=flops, bytes_accessed=nbytes, transcendentals=0),
    )(*args)


def struct(dtype, *shape):
    return jax.ShapeDtypeStruct(shape, dtype)


def halves(row):
    v = row.astype(F32)
    blank = jnp.zeros((v.shape[0], 2 * LANES - v.shape[1]), F32)
    return v[:, :LANES], jnp.concatenate([v[:, LANES:], blank], axis=1)


def edges_kernel(core_ref, field_ref, near_ref, far_ref):
    rows, channels, cols = field_ref.shape
    lane = lax.broadcasted_iota(jnp.int32, (channels, LANES), 1)
    first = core_ref[0] == 0
    for g in range(3):
        head = jnp.zeros((channels, LANES), F32)
        tail = jnp.zeros((channels, LANES), F32)
        for m in range(min(6, rows - 6 * g)):
            low, high = halves(field_ref[g * 6 + m])
            inside = (lane >= HMAX * m) & (lane < HMAX * (m + 1))
            low = pltpu.roll(low, HMAX * m, 1) if m else low
            high = pltpu.roll(high, (HMAX * m - (cols - HMAX - LANES)) % LANES, 1)
            head = jnp.where(inside, low, head)
            tail = jnp.where(inside, high, tail)
        near_ref[g] = jnp.where(first, tail, head).astype(BF16)
        far_ref[g] = jnp.where(first, head, tail).astype(BF16)


def widened(row, left, right, m):
    cols = row.shape[1]
    edge = HMAX + cols - LANES
    lane = lax.broadcasted_iota(jnp.int32, left.shape, 1)
    low, high = (pltpu.roll(v, HMAX, 1) for v in halves(row))
    before = pltpu.roll(left, (-HMAX * m) % LANES, 1) if m else left
    after = pltpu.roll(right, (edge - HMAX * m) % LANES, 1)
    one = jnp.where(lane < HMAX, before, low)
    two = jnp.where(lane < HMAX, low, high)
    return one, jnp.where(lane < edge, two, jnp.where(lane < edge + HMAX, after, 0.0))


def sides(core_ref, near, far):
    near, far = near.astype(F32), far.astype(F32)
    first = core_ref[0] == 0
    return jnp.where(first, far, near), jnp.where(first, near, far)


def rows_kernel(core_ref, even_ref, field_ref, near_ref, far_ref, one_ref, two_ref):
    rows = field_ref.shape[0]
    ends = []
    for r in (0, rows - 1):
        left, right = sides(core_ref, near_ref[r // 6], far_ref[r // 6])
        ends.append(jnp.concatenate(widened(field_ref[r], left, right, r % 6), axis=1))
    even = even_ref[0] == 1
    one_ref[0] = jnp.where(even, ends[1], ends[0]).astype(BF16)
    two_ref[0] = jnp.where(even, ends[0], ends[1]).astype(BF16)


def toeplitz_kernel(
    core_ref, even_ref, field_ref, near_ref, far_ref, one_ref, two_ref, base_ref, weight_ref,
    out_ref, ext_ref, rest_ref, band_ref,
):
    rows, channels, cols = field_ref.shape
    lane = lax.broadcasted_iota(jnp.int32, (channels, LANES), 1)
    even = even_ref[0] == 1
    for r in range(rows + 2):
        if r in (0, rows + 1):
            a, b = (one_ref, two_ref) if r else (two_ref, one_ref)
            row = jnp.where(even, a[0].astype(F32), b[0].astype(F32))
            one, two = row[:, :LANES], row[:, LANES:]
        else:
            g, m = divmod(r - 1, 6)
            left, right = sides(core_ref, near_ref[g], far_ref[g])
            one, two = widened(field_ref[r - 1], left, right, m)
        ext_ref[r, :, :LANES] = one.astype(BF16)
        ext_ref[r, :, LANES:] = two.astype(BF16)
        for a in range(3):
            i = r - a
            if 0 <= i < rows:
                part = pltpu.roll(two, 2 * HMAX * a, 1) if a else two
                inside = (lane >= 2 * HMAX * a) & (lane < 2 * HMAX * (a + 1))
                rest_ref[i] = jnp.where(inside, part, rest_ref[i] if a else 0.0)

    r = lax.broadcasted_iota(jnp.int32, (LANES, LANES), 0)
    s = lax.broadcasted_iota(jnp.int32, (LANES, LANES), 1)

    @pl.loop(0, rows)
    def _(row):
        for k in range(BASES):
            cols_k = slice(k * LANES, (k + 1) * LANES)
            spill = []
            for a in range(3):
                line = base_ref[row, k * 3 + a : k * 3 + a + 1, :]
                circ = pltpu.roll(
                    jnp.broadcast_to(line, (LANES, LANES)), 0, 1, stride=1, stride_axis=0
                )
                band_ref[a * LANES : (a + 1) * LANES, cols_k] = jnp.where(s <= r, circ, 0.0).astype(
                    BF16
                )
                spill.append(jnp.where(s > r, circ, 0.0)[: 2 * HMAX])
            spill.append(jnp.zeros((LANES - 6 * HMAX, LANES), F32))
            band_ref[3 * LANES :, cols_k] = jnp.concatenate(spill, axis=0).astype(BF16)
        lines = [ext_ref[row + a] for a in range(3)]
        upper = [v[:, :LANES] for v in lines] + [rest_ref[row].astype(BF16)]
        lower = [v[:, LANES:] for v in lines] + [jnp.zeros((channels, LANES), BF16)]
        lhs = jnp.concatenate(
            [jnp.concatenate(upper, axis=1), jnp.concatenate(lower, axis=1)], axis=0
        )
        sums = jnp.dot(lhs, band_ref[...], preferred_element_type=F32).astype(BF16)
        stacked = jnp.concatenate(
            [
                jnp.concatenate(
                    [
                        sums[u * channels : (u + 1) * channels, k * LANES : (k + 1) * LANES]
                        for u in range(2)
                    ],
                    axis=1,
                )
                for k in range(BASES)
            ],
            axis=0,
        )
        mixed = jnp.dot(weight_ref[...], stacked, preferred_element_type=F32)
        out_ref[row] = mixed[:, :cols]


def halo(field):
    channels = field.shape[1]
    core = lax.axis_index("core").reshape(1)
    even = (1 - lax.axis_index("x") % 2).reshape(1)
    near_pairs = [(i, i ^ 1) for i in range(16)]
    far_pairs = [(i, (i + 1) % 16 if i % 2 else (i - 1) % 16) for i in range(16)]
    lat = ("zl", "x")
    even_pairs = [(i, i ^ 1) for i in range(32)]
    odd_pairs = [(i, i + 1 if i % 2 else i - 1) for i in range(1, 31)]
    packed = struct(BF16, 3, channels, LANES)
    near, far = call(edges_kernel, (packed, packed), core, field, smem=1)
    far = lax.ppermute(far, LON, far_pairs)
    near, far = lax.optimization_barrier((near, far))
    near = lax.ppermute(near, LON, near_pairs)
    row = struct(BF16, 1, channels, 2 * LANES)
    one, two = call(rows_kernel, (row, row), core, even, field, near, far, smem=2)
    one = lax.ppermute(one, lat, even_pairs)
    two = lax.ppermute(two, lat, odd_pairs)
    return core, even, near, far, one, two


def disco(field, around, disco_reach, disco_taps, disco_weight):
    lat_rows, channels, lon_cols = field.shape
    core, even, near, far, one, two = around
    offsets = jnp.abs(jnp.arange(TAPS, dtype=jnp.int32) - HMAX)
    within = offsets[None, :] <= disco_reach[:, None]
    coef = jnp.where(
        within[:, None, :], disco_taps.reshape(lat_rows, BASES * 3, TAPS), 0.0
    )
    base = jnp.concatenate(
        [
            coef[:, :, :1],
            jnp.zeros((lat_rows, BASES * 3, LANES - TAPS), F32),
            coef[:, :, :0:-1],
        ],
        axis=2,
    )
    weight = disco_weight.transpose(2, 0, 1).reshape(channels, BASES * channels)
    return call(
        toeplitz_kernel,
        struct(F32, lat_rows, channels, lon_cols),
        core,
        even,
        field,
        near,
        far,
        one,
        two,
        base,
        weight,
        smem=2,
        flops=2 * lat_rows * 128 * 512 * 512,
        scratch=[
            pltpu.VMEM((lat_rows + 2, channels, 2 * LANES), BF16),
            pltpu.VMEM((lat_rows, channels, LANES), F32),
            pltpu.VMEM((4 * LANES, BASES * LANES), BF16),
        ],
    )


def exchange(cells, axes):
    return lax.all_to_all(cells, axes, split_axis=0, concat_axis=0, tiled=True)


def per_device(grid_field, disco_reach, disco_taps, disco_weight, legendre, mixing):
    lat_rows, lon_cols, channels = grid_field.shape
    wide = 2 * channels
    own = mixing.shape[0]
    place = lax.axis_index(LON)
    field = grid_field.transpose(0, 2, 1)
    forward = jnp.asarray(table(lon_cols, 1.0 / math.sqrt(NLON)))
    forward = lax.dynamic_index_in_dim(forward, place, 0, keepdims=False)
    inverse = jnp.asarray(table(lon_cols, 1.0 / math.sqrt(MODES)))
    inverse = lax.dynamic_index_in_dim(inverse, place, 0, keepdims=False)
    spread = [pltpu.VMEM((MODES * lat_rows, wide), F32)]

    waves = call(
        forward_kernel, struct(BF16, 16, 2 * lat_rows, wide), field, forward, scratch=spread
    )
    degrees = jnp.arange(legendre.shape[2], dtype=jnp.int32)
    orders = place * 2 + jnp.arange(2, dtype=jnp.int32)
    masked = jnp.where(degrees[None, None, :] >= orders[None, :, None], legendre, jnp.zeros((), BF16))
    masked = masked.reshape(lat_rows, 2, 8, 4, own).transpose(3, 1, 0, 2, 4)
    masked = masked.reshape(4, 2 * lat_rows, 8 * own)
    masked = jnp.pad(masked, ((0, 0), (0, 0), (0, 256 - 8 * own)))
    weight = jnp.concatenate([mixing[:, 0], mixing[:, 1]], axis=2)

    core, even, near, far, one, two = halo(field)
    waves = exchange(waves, LON)
    message = call(spectra_kernel, struct(BF16, 4, 2 * lat_rows, 384), waves, masked)
    message = exchange(message, ("x",))
    message, near = lax.optimization_barrier((message, near))
    coeffs, leg = call(
        analysis_kernel,
        (struct(BF16, 8, 2 * own, wide), struct(BF16, 2, 4 * lat_rows, 256)),
        message,
    )
    coeffs = exchange(coeffs, ("zl",))
    mixed = call(mixing_kernel, struct(BF16, 8, 2 * own, wide), coeffs, weight)
    mixed = exchange(mixed, ("zl",))
    mixed, one, two = lax.optimization_barrier((mixed, one, two))
    parts = call(synthesis_kernel, struct(BF16, 4, 2 * lat_rows, wide), mixed, leg)
    parts = exchange(parts, ("x",))
    modes = call(modes_kernel, struct(BF16, 16, 2 * lat_rows, wide), parts)
    modes = exchange(modes, LON)
    disco_out = disco(field, (core, even, near, far, one, two), disco_reach, disco_taps, disco_weight)
    out = call(
        final_kernel,
        struct(BF16, lat_rows, channels, lon_cols),
        modes,
        inverse,
        disco_out,
        field,
        scratch=spread,
    )
    return out.transpose(0, 2, 1)


def solution(mesh):
    fine = Mesh(mesh.devices.reshape(8, 4, 4, 2, 2), ("zl", "x", "y", "zh", "core"))
    lat, lon = ("zl", "x"), LON
    in_specs = (
        P(lat, lon, None),
        P(lat),
        P(lat, None),
        P(),
        P(lat, lon, None),
        P(lat, None, None, None),
    )
    return jax.shard_map(
        per_device, mesh=fine, in_specs=in_specs, out_specs=P(lat, lon, None), check_vma=False
    )
```

```python
import math

import jax
import jax.numpy as jnp
import numpy as np
from jax import lax
from jax.experimental import pallas as pl
from jax.experimental.pallas import tpu as pltpu
from jax.sharding import Mesh
from jax.sharding import PartitionSpec as P

NLON = 2880
MODES = 32
HMAX = 20
TAPS = 2 * HMAX + 1
BASES = 4
LANES = 128
BF16 = jnp.bfloat16
F32 = jnp.float32
LON = ("y", "zh", "core")


def pair_of(sector):
    return (sector + 15) % 16 // 2


def member(pair, m):
    return (2 * pair + 1 + m) % 16


def orders_at(zh):
    out = []
    for group in range(8):
        pair = pair_of(group // 2 * 4 + zh * 2 + group % 2)
        out += [member(pair, m) * 2 + odd for m in range(2) for odd in range(2)]
    return np.array(out)


def table(lon_cols, scale):
    sectors = []
    for sector in range(NLON // lon_cols):
        columns = sector * lon_cols + np.arange(lon_cols)
        residues = (orders_at(sector // 2 % 2)[:, None] * columns[None, :]) % NLON
        phases = residues.astype(np.float32) * np.float32(2.0 * math.pi / NLON)
        sectors.append(np.concatenate([np.cos(phases), -np.sin(phases)], axis=0))
    return (np.stack(sectors).astype(np.float32) * np.float32(scale)).astype(BF16)


def degree_order():
    out = np.zeros((768, 256), np.float32)
    for o in range(192):
        out[o // 24 * 96 + o % 24, o] = 1.0
    return out.astype(BF16)


def first_half(shape):
    return lax.broadcasted_iota(jnp.int32, shape, len(shape) - 1) < 64


def forward_kernel(field_ref, table_ref, out_ref, rows_ref):
    rows = field_ref.shape[0]
    field = field_ref[...].reshape(rows * 64, field_ref.shape[2])
    waves = lax.dot_general(
        table_ref[...], field, (((1,), (1,)), ((), ())), preferred_element_type=F32
    )
    half = first_half((MODES, LANES))
    for m in range(rows // 2):
        re = waves[:MODES, m * LANES : (m + 1) * LANES]
        im = waves[MODES:, m * LANES : (m + 1) * LANES]
        rows_ref[pl.ds(2 * m, MODES, stride=rows), :] = jnp.where(half, re, pltpu.roll(im, 64, 1))
        rows_ref[pl.ds(2 * m + 1, MODES, stride=rows), :] = jnp.where(
            half, pltpu.roll(re, 64, 1), im
        )
    out_ref[...] = rows_ref[...].astype(BF16).reshape(out_ref.shape)


def spectra_kernel(waves_ref, legs_ref, out_ref):
    total = waves_ref[0].astype(F32)
    for n in range(1, waves_ref.shape[0]):
        total += waves_ref[n].astype(F32)
    spectra = total.astype(BF16)
    for x in range(4):
        out_ref[x, :, :LANES] = spectra
        out_ref[x, :, LANES:] = legs_ref[x]


def legs_kernel(orders_ref, own_ref, other_ref, pick_ref, out_ref, lines_ref):
    row = lax.broadcasted_iota(jnp.int32, (32, LANES), 0)
    degree = lax.broadcasted_iota(jnp.int32, (32, LANES), 1)
    sides = []
    for side, ref in enumerate((own_ref, other_ref)):
        tiles = [ref[3 + n, t * 32 : (t + 1) * 32, :].astype(F32) for n in range(3) for t in range(2)]
        tiles[0] = jnp.where(degree >= orders_ref[side] + row % 2, tiles[0], 0.0)
        sides.append(jnp.concatenate(tiles, axis=1))
    lines = jnp.concatenate(sides, axis=0)
    turned = [lines] + [pltpu.roll(lines, 768 - 24 * x, 1) for x in range(1, 4)]
    turned = jnp.concatenate(turned, axis=0).astype(BF16)
    picked = jnp.dot(turned, pick_ref[...], preferred_element_type=F32)
    for t in range(2):
        lines_ref[t] = picked[:, t * LANES : (t + 1) * LANES]
    for side in range(2):
        m = orders_ref[2] if side == 0 else 1 - orders_ref[2]
        for q in range(2):
            at = pl.multiple_of((m * 2 + q) * 16, 16)
            for x in range(4):
                for t in range(2):
                    v = lines_ref[t, pl.ds(x * 64 + side * 32 + q, 16, stride=2), :]
                    out_ref[x, pl.ds(at, 16), t * LANES : (t + 1) * LANES] = v.astype(BF16)


def analysis_kernel(got_ref, coeff_ref, leg_ref):
    for m in range(2):
        parts = []
        for q in range(2):
            n = m * 2 + q
            both = jnp.concatenate([got_ref[x, n * 16 : (n + 1) * 16, :] for x in range(4)], axis=0)
            leg_ref[n] = both[:, LANES:]
            parts.append(
                lax.dot_general(
                    both[:, LANES:],
                    both[:, :LANES],
                    (((0,), (0,)), ((), ())),
                    preferred_element_type=F32,
                )
            )
        for n in range(8):
            rows = jnp.concatenate([p[n * 24 : (n + 1) * 24] for p in parts], axis=0)
            coeff_ref[m * 8 + n] = rows.astype(BF16)


def mixing_kernel(coeff_ref, weight_ref, out_ref):
    total = coeff_ref[0].astype(F32)
    for n in range(1, coeff_ref.shape[0]):
        total += coeff_ref[n].astype(F32)
    lhs = jnp.concatenate([total[:, :64], total[:, 64:]], axis=0).astype(BF16)
    degree = lax.broadcasted_iota(jnp.int32, (96, LANES), 0) % 24
    acc = jnp.zeros((96, LANES), F32)
    for l in range(24):
        acc = jnp.where(
            degree == l, jnp.dot(lhs, weight_ref[l], preferred_element_type=F32), acc
        )
    turned = pltpu.roll(acc[48:], 64, 1)
    mixed = acc[:48] + jnp.where(first_half((48, LANES)), -turned, turned)
    mixed = mixed.astype(BF16)
    for n in range(out_ref.shape[0]):
        out_ref[n] = mixed


def synthesis_kernel(mixed_ref, leg_ref, out_ref):
    for m in range(2):
        blocks = [mixed_ref[m * 8 + n].astype(F32) for n in range(8)]
        for q in range(2):
            at = m * 2 + q
            mixed = jnp.concatenate([v[q * 24 : (q + 1) * 24] for v in blocks], axis=0)
            modes = jnp.dot(
                leg_ref[at][:, :192], mixed.astype(BF16), preferred_element_type=F32
            ).astype(BF16)
            for x in range(4):
                for g in range(8):
                    out_ref[x * 8 + g, at * 16 : (at + 1) * 16, :] = modes[x * 16 : (x + 1) * 16]


def final_kernel(modes_ref, table_ref, disco_ref, field_ref, out_ref, rows_ref):
    rows, channels, cols = field_ref.shape
    for g in range(8):
        total = modes_ref[g].astype(F32)
        for x in range(1, 4):
            total += modes_ref[x * 8 + g].astype(F32)
        rows_ref[g * 64 : (g + 1) * 64, :] = total
    half = first_half((MODES, LANES))
    for m in range(rows // 2):
        one = rows_ref[pl.ds(2 * m, MODES, stride=rows), :]
        two = rows_ref[pl.ds(2 * m + 1, MODES, stride=rows), :]
        re = jnp.where(half, one, pltpu.roll(two, 64, 1))
        im = jnp.where(half, pltpu.roll(one, 64, 1), two)
        spectral = lax.dot_general(
            jnp.concatenate([re, im], axis=0).astype(BF16),
            table_ref[...],
            (((0,), (0,)), ((), ())),
            preferred_element_type=F32,
        ).astype(BF16)
        for u in range(2):
            v = spectral[u * 64 : (u + 1) * 64].astype(F32) + disco_ref[2 * m + u]
            inner = math.sqrt(2.0 / math.pi) * (v + 0.044715 * (v * v * v))
            act = 0.5 * v * (1.0 + jnp.tanh(inner))
            out_ref[2 * m + u] = (field_ref[2 * m + u].astype(F32) + act).astype(BF16)


def call(kernel, out, *args, scratch=(), flops=10**7, smem=0):
    nbytes = sum(a.size * a.dtype.itemsize for a in args)
    vmem = pl.BlockSpec(memory_space=pltpu.VMEM)
    scalar = pl.BlockSpec(memory_space=pltpu.SMEM)
    return pl.pallas_call(
        kernel,
        out_shape=out,
        in_specs=[scalar] * smem + [vmem] * (len(args) - smem),
        out_specs=jax.tree.map(lambda _: vmem, out),
        scratch_shapes=scratch,
        compiler_params=pltpu.CompilerParams(vmem_limit_bytes=16 * 2**20),
        cost_estimate=pl.CostEstimate(flops=flops, bytes_accessed=nbytes, transcendentals=0),
    )(*args)


def struct(dtype, *shape):
    return jax.ShapeDtypeStruct(shape, dtype)


def halves(row):
    v = row.astype(F32)
    blank = jnp.zeros((v.shape[0], 2 * LANES - v.shape[1]), F32)
    return v[:, :LANES], jnp.concatenate([v[:, LANES:], blank], axis=1)


def edges_kernel(core_ref, field_ref, leg_ref, near_ref, far_ref, lines_ref):
    for i in range(leg_ref.shape[0]):
        lines_ref[2 * i : 2 * i + 2, :] = leg_ref[i].astype(F32)
    for n in range(3):
        for t in range(2):
            at = (2 * n + t) * LANES
            far_ref[3 + n, t * 32 : (t + 1) * 32, :] = lines_ref[:, at : at + LANES].astype(BF16)
    rows, channels, cols = field_ref.shape
    lane = lax.broadcasted_iota(jnp.int32, (channels, LANES), 1)
    first = core_ref[0] == 0
    for g in range(3):
        head = jnp.zeros((channels, LANES), F32)
        tail = jnp.zeros((channels, LANES), F32)
        for m in range(min(6, rows - 6 * g)):
            low, high = halves(field_ref[g * 6 + m])
            inside = (lane >= HMAX * m) & (lane < HMAX * (m + 1))
            low = pltpu.roll(low, HMAX * m, 1) if m else low
            high = pltpu.roll(high, (HMAX * m - (cols - HMAX - LANES)) % LANES, 1)
            head = jnp.where(inside, low, head)
            tail = jnp.where(inside, high, tail)
        near_ref[g] = jnp.where(first, tail, head).astype(BF16)
        far_ref[g] = jnp.where(first, head, tail).astype(BF16)


def widened(row, left, right, m):
    cols = row.shape[1]
    edge = HMAX + cols - LANES
    lane = lax.broadcasted_iota(jnp.int32, left.shape, 1)
    low, high = (pltpu.roll(v, HMAX, 1) for v in halves(row))
    before = pltpu.roll(left, (-HMAX * m) % LANES, 1) if m else left
    after = pltpu.roll(right, (edge - HMAX * m) % LANES, 1)
    one = jnp.where(lane < HMAX, before, low)
    two = jnp.where(lane < HMAX, low, high)
    return one, jnp.where(lane < edge, two, jnp.where(lane < edge + HMAX, after, 0.0))


def sides(core_ref, near, far):
    near, far = near.astype(F32), far.astype(F32)
    first = core_ref[0] == 0
    return jnp.where(first, far, near), jnp.where(first, near, far)


def rows_kernel(core_ref, even_ref, field_ref, near_ref, far_ref, one_ref, two_ref):
    rows = field_ref.shape[0]
    ends = []
    for r in (0, rows - 1):
        left, right = sides(core_ref, near_ref[r // 6], far_ref[r // 6])
        ends.append(jnp.concatenate(widened(field_ref[r], left, right, r % 6), axis=1))
    even = even_ref[0] == 1
    one_ref[0] = jnp.where(even, ends[1], ends[0]).astype(BF16)
    two_ref[0] = jnp.where(even, ends[0], ends[1]).astype(BF16)


def toeplitz_kernel(
    core_ref, even_ref, field_ref, near_ref, far_ref, one_ref, two_ref, base_ref, weight_ref,
    out_ref, ext_ref, rest_ref, band_ref,
):
    rows, channels, cols = field_ref.shape
    lane = lax.broadcasted_iota(jnp.int32, (channels, LANES), 1)
    even = even_ref[0] == 1
    for r in range(rows + 2):
        if r in (0, rows + 1):
            a, b = (one_ref, two_ref) if r else (two_ref, one_ref)
            row = jnp.where(even, a[0].astype(F32), b[0].astype(F32))
            one, two = row[:, :LANES], row[:, LANES:]
        else:
            g, m = divmod(r - 1, 6)
            left, right = sides(core_ref, near_ref[g], far_ref[g])
            one, two = widened(field_ref[r - 1], left, right, m)
        ext_ref[r, :, :LANES] = one.astype(BF16)
        ext_ref[r, :, LANES:] = two.astype(BF16)
        for a in range(3):
            i = r - a
            if 0 <= i < rows:
                part = pltpu.roll(two, 2 * HMAX * a, 1) if a else two
                inside = (lane >= 2 * HMAX * a) & (lane < 2 * HMAX * (a + 1))
                rest_ref[i] = jnp.where(inside, part, rest_ref[i] if a else 0.0)

    r = lax.broadcasted_iota(jnp.int32, (LANES, LANES), 0)
    s = lax.broadcasted_iota(jnp.int32, (LANES, LANES), 1)

    @pl.loop(0, rows)
    def _(row):
        for k in range(BASES):
            cols_k = slice(k * LANES, (k + 1) * LANES)
            spill = []
            for a in range(3):
                line = base_ref[row, k * 3 + a : k * 3 + a + 1, :]
                circ = pltpu.roll(
                    jnp.broadcast_to(line, (LANES, LANES)), 0, 1, stride=1, stride_axis=0
                )
                band_ref[a * LANES : (a + 1) * LANES, cols_k] = jnp.where(s <= r, circ, 0.0).astype(
                    BF16
                )
                spill.append(jnp.where(s > r, circ, 0.0)[: 2 * HMAX])
            spill.append(jnp.zeros((LANES - 6 * HMAX, LANES), F32))
            band_ref[3 * LANES :, cols_k] = jnp.concatenate(spill, axis=0).astype(BF16)
        lines = [ext_ref[row + a] for a in range(3)]
        upper = [v[:, :LANES] for v in lines] + [rest_ref[row].astype(BF16)]
        lower = [v[:, LANES:] for v in lines] + [jnp.zeros((channels, LANES), BF16)]
        lhs = jnp.concatenate(
            [jnp.concatenate(upper, axis=1), jnp.concatenate(lower, axis=1)], axis=0
        )
        sums = jnp.dot(lhs, band_ref[...], preferred_element_type=F32).astype(BF16)
        stacked = jnp.concatenate(
            [
                jnp.concatenate(
                    [
                        sums[u * channels : (u + 1) * channels, k * LANES : (k + 1) * LANES]
                        for u in range(2)
                    ],
                    axis=1,
                )
                for k in range(BASES)
            ],
            axis=0,
        )
        mixed = jnp.dot(weight_ref[...], stacked, preferred_element_type=F32)
        out_ref[row] = mixed[:, :cols]


def lat_rows_of(field, scalars, near, far):
    row = struct(BF16, 1, field.shape[1], 2 * LANES)
    one, two = call(rows_kernel, (row, row), *scalars, field, near, far, smem=2)
    lat = ("zl", "x")
    one = lax.ppermute(one, lat, [(i, i ^ 1) for i in range(32)])
    two = lax.ppermute(two, lat, [(i, i + 1 if i % 2 else i - 1) for i in range(1, 31)])
    return one, two


def disco(field, around, disco_reach, disco_taps, disco_weight):
    lat_rows, channels, lon_cols = field.shape
    core, even, near, far, one, two = around
    offsets = jnp.abs(jnp.arange(TAPS, dtype=jnp.int32) - HMAX)
    within = offsets[None, :] <= disco_reach[:, None]
    coef = jnp.where(
        within[:, None, :], disco_taps.reshape(lat_rows, BASES * 3, TAPS), 0.0
    )
    base = jnp.concatenate(
        [
            coef[:, :, :1],
            jnp.zeros((lat_rows, BASES * 3, LANES - TAPS), F32),
            coef[:, :, :0:-1],
        ],
        axis=2,
    )
    weight = disco_weight.transpose(2, 0, 1).reshape(channels, BASES * channels)
    return call(
        toeplitz_kernel,
        struct(F32, lat_rows, channels, lon_cols),
        core,
        even,
        field,
        near,
        far,
        one,
        two,
        base,
        weight,
        smem=2,
        flops=2 * lat_rows * 128 * 512 * 512,
        scratch=[
            pltpu.VMEM((lat_rows + 2, channels, 2 * LANES), BF16),
            pltpu.VMEM((lat_rows, channels, LANES), F32),
            pltpu.VMEM((4 * LANES, BASES * LANES), BF16),
        ],
    )


def exchange(cells, axes):
    return lax.all_to_all(cells, axes, split_axis=0, concat_axis=0, tiled=True)


def line_exchange(cells):
    groups = [
        [zl * 16 + member(pair, m) for m in range(2) for zl in range(8)] for pair in range(8)
    ]
    return lax.all_to_all(
        cells, ("zl", *LON), split_axis=0, concat_axis=0, tiled=True, axis_index_groups=groups
    )


def per_device(grid_field, disco_reach, disco_taps, disco_weight, legendre, mixing):
    lat_rows, lon_cols, channels = grid_field.shape
    wide = 2 * channels
    own = mixing.shape[0]
    place = lax.axis_index(LON)
    field = grid_field.transpose(0, 2, 1)
    forward = jnp.asarray(table(lon_cols, 1.0 / math.sqrt(NLON)))
    forward = lax.dynamic_index_in_dim(forward, place, 0, keepdims=False)
    inverse = jnp.asarray(table(lon_cols, 1.0 / math.sqrt(MODES)))
    inverse = lax.dynamic_index_in_dim(inverse, place, 0, keepdims=False)
    spread = [pltpu.VMEM((MODES * lat_rows, wide), F32)]

    core = lax.axis_index("core").reshape(1)
    even = (1 - lax.axis_index("x") % 2).reshape(1)
    packed = struct(BF16, 3, channels, LANES)
    near, mine = call(
        edges_kernel,
        (packed, struct(BF16, 6, channels, LANES)),
        core,
        field,
        legendre,
        smem=1,
        scratch=[pltpu.VMEM((2 * lat_rows, 768), F32)],
    )
    swap = [(i, member(pair_of(i), i % 2)) for i in range(16)]
    far = lax.ppermute(mine, LON, swap)
    lines, mine = lax.optimization_barrier((field, mine))
    waves = call(
        forward_kernel,
        struct(BF16, 8, 4 * lat_rows, wide),
        lines,
        forward,
        scratch=spread,
        flops=10**7,
    )
    waves = exchange(waves, ("y", "core"))
    waves, near = lax.optimization_barrier((waves, near))
    pair = pair_of(place)
    mate = 1 - core[0]
    orders = jnp.stack([member(pair, mate) * 2, member(pair, 1 - mate) * 2, mate])
    weight = jnp.concatenate([mixing[:, 0], mixing[:, 1]], axis=2)
    legs = call(
        legs_kernel,
        struct(BF16, 4, 4 * lat_rows, 256),
        orders.astype(jnp.int32),
        mine,
        far,
        jnp.asarray(degree_order()),
        smem=1,
        flops=10**7,
        scratch=[pltpu.VMEM((2, 16 * lat_rows, LANES), F32)],
    )
    message = call(spectra_kernel, struct(BF16, 4, 4 * lat_rows, 384), waves, legs)
    message = exchange(message, ("x",))
    near = lax.ppermute(near, LON, [(i, i ^ 1) for i in range(16)])
    message, near = lax.optimization_barrier((message, near))
    coeffs, leg = call(
        analysis_kernel,
        (struct(BF16, 16, 2 * own, wide), struct(BF16, 4, 4 * lat_rows, 256)),
        message,
    )
    coeffs = line_exchange(coeffs)
    one, two = lat_rows_of(field, (core, even), near, far)
    coeffs, one, two = lax.optimization_barrier((coeffs, one, two))
    mixed = call(mixing_kernel, struct(BF16, 16, 2 * own, wide), coeffs, weight)
    mixed = line_exchange(mixed)
    disco_out = disco(field, (core, even, near, far, one, two), disco_reach, disco_taps, disco_weight)
    mixed, disco_out = lax.optimization_barrier((mixed, disco_out))
    modes = call(synthesis_kernel, struct(BF16, 32, 4 * lat_rows, wide), mixed, leg)
    modes = exchange(modes, ("x", "y", "core"))
    out = call(
        final_kernel,
        struct(BF16, lat_rows, channels, lon_cols),
        modes,
        inverse,
        disco_out,
        field,
        scratch=spread,
    )
    return out.transpose(0, 2, 1)


def solution(mesh):
    fine = Mesh(mesh.devices.reshape(8, 4, 4, 2, 2), ("zl", "x", "y", "zh", "core"))
    lat, lon = ("zl", "x"), LON
    in_specs = (
        P(lat, lon, None),
        P(lat),
        P(lat, None),
        P(),
        P(lat, lon, None),
        P(lat, None, None, None),
    )
    return jax.shard_map(
        per_device, mesh=fine, in_specs=in_specs, out_specs=P(lat, lon, None), check_vma=False
    )
```

```python
import math

import jax
import jax.numpy as jnp
import numpy as np
from jax import lax
from jax.experimental import pallas as pl
from jax.experimental.pallas import tpu as pltpu
from jax.sharding import Mesh
from jax.sharding import PartitionSpec as P

NLON = 2880
MODES = 32
HMAX = 20
TAPS = 2 * HMAX + 1
BASES = 4
LANES = 128
BF16 = jnp.bfloat16
F32 = jnp.float32
LON = ("y", "zh", "core")
EARLY = (1, 4)


def pair_of(sector):
    return (sector + 15) % 16 // 2


def member(pair, m):
    return (2 * pair + 1 + m) % 16


def orders_at(zh):
    out = []
    for group in range(8):
        pair = pair_of(group // 2 * 4 + zh * 2 + group % 2)
        out += [member(pair, m) * 2 + odd for m in range(2) for odd in range(2)]
    return np.array(out)


def table(lon_cols, scale, orders_of):
    sectors = []
    for sector in range(NLON // lon_cols):
        columns = sector * lon_cols + np.arange(lon_cols)
        residues = (orders_of(sector)[:, None] * columns[None, :]) % NLON
        phases = residues.astype(np.float32) * np.float32(2.0 * math.pi / NLON)
        sectors.append(np.concatenate([np.cos(phases), -np.sin(phases)], axis=0))
    return (np.stack(sectors).astype(np.float32) * np.float32(scale)).astype(BF16)


def degree_order():
    out = np.zeros((768, 256), np.float32)
    for o in range(192):
        out[o // 24 * 96 + o % 24, o] = 1.0
    return out.astype(BF16)


def first_half(shape):
    return lax.broadcasted_iota(jnp.int32, shape, len(shape) - 1) < 64


def forward_kernel(field_ref, table_ref, out_ref, rows_ref):
    rows = field_ref.shape[0]
    field = field_ref[...].reshape(rows * 64, field_ref.shape[2])
    waves = lax.dot_general(
        table_ref[...], field, (((1,), (1,)), ((), ())), preferred_element_type=F32
    )
    half = first_half((MODES, LANES))
    for m in range(rows // 2):
        re = waves[:MODES, m * LANES : (m + 1) * LANES]
        im = waves[MODES:, m * LANES : (m + 1) * LANES]
        rows_ref[pl.ds(2 * m, MODES, stride=rows), :] = jnp.where(half, re, pltpu.roll(im, 64, 1))
        rows_ref[pl.ds(2 * m + 1, MODES, stride=rows), :] = jnp.where(
            half, pltpu.roll(re, 64, 1), im
        )
    out_ref[...] = rows_ref[...].astype(BF16).reshape(out_ref.shape)


def spectra_kernel(waves_ref, legs_ref, out_ref):
    total = waves_ref[0].astype(F32)
    for n in range(1, waves_ref.shape[0]):
        total += waves_ref[n].astype(F32)
    spectra = total.astype(BF16)
    for x in range(4):
        out_ref[x, :, :LANES] = spectra
        out_ref[x, :, LANES:] = legs_ref[x]


def legs_kernel(orders_ref, leg_ref, pick_ref, out_ref, rows_ref, lines_ref):
    rows = leg_ref.shape[0]
    for i in range(rows):
        rows_ref[2 * i : 2 * i + 2, :] = leg_ref[i].astype(F32)
    row = lax.broadcasted_iota(jnp.int32, (2 * rows, LANES), 0)
    degree = lax.broadcasted_iota(jnp.int32, (2 * rows, LANES), 1)
    low = jnp.where(degree >= orders_ref[0] + row % 2, rows_ref[:, :LANES], 0.0)
    lines = jnp.concatenate([low, rows_ref[:, LANES:]], axis=1)
    turned = [lines] + [pltpu.roll(lines, 768 - 24 * x, 1) for x in range(1, 4)]
    turned = jnp.concatenate(turned, axis=0).astype(BF16)
    picked = jnp.dot(turned, pick_ref[...], preferred_element_type=F32)
    for t in range(2):
        lines_ref[t] = picked[:, t * LANES : (t + 1) * LANES]
    for q in range(2):
        for x in range(4):
            for t in range(2):
                v = lines_ref[t, pl.ds(x * 2 * rows + q, rows, stride=2), :]
                out_ref[x, q * rows : (q + 1) * rows, t * LANES : (t + 1) * LANES] = v.astype(BF16)


def analysis_kernel(got_ref, far_ref, coeff_ref, leg_ref, pack_ref):
    parts = []
    for q in range(2):
        both = jnp.concatenate([got_ref[x, q * 16 : (q + 1) * 16, :] for x in range(4)], axis=0)
        leg_ref[q] = both[:, LANES:]
        for t in range(2):
            pack_ref[3 + 2 * q + t] = both[:, (t + 1) * LANES : (t + 2) * LANES]
        parts.append(
            lax.dot_general(
                both[:, LANES:],
                both[:, :LANES],
                (((0,), (0,)), ((), ())),
                preferred_element_type=F32,
            )
        )
    for n in range(8):
        rows = jnp.concatenate([p[n * 24 : (n + 1) * 24] for p in parts], axis=0)
        coeff_ref[n] = rows.astype(BF16)
    for n in range(3):
        pack_ref[n] = far_ref[n]


def mixing_kernel(coeff_ref, weight_ref, out_ref):
    total = coeff_ref[0].astype(F32)
    for n in range(1, coeff_ref.shape[0]):
        total += coeff_ref[n].astype(F32)
    lhs = jnp.concatenate([total[:, :64], total[:, 64:]], axis=0).astype(BF16)
    degree = lax.broadcasted_iota(jnp.int32, (96, LANES), 0) % 24
    acc = jnp.zeros((96, LANES), F32)
    for l in range(24):
        acc = jnp.where(
            degree == l, jnp.dot(lhs, weight_ref[l], preferred_element_type=F32), acc
        )
    turned = pltpu.roll(acc[48:], 64, 1)
    mixed = acc[:48] + jnp.where(first_half((48, LANES)), -turned, turned)
    mixed = mixed.astype(BF16)
    for n in range(out_ref.shape[0]):
        out_ref[n] = mixed


def synthesis_kernel(mate_ref, mixed_ref, own_ref, other_ref, out_ref):
    for side in range(2):
        m = mate_ref[0] if side == 0 else 1 - mate_ref[0]
        blocks = [mixed_ref[m * 8 + n].astype(F32) for n in range(8)]
        for q in range(2):
            if side == 0:
                leg = own_ref[q]
            else:
                leg = jnp.concatenate([other_ref[3 + 2 * q], other_ref[4 + 2 * q]], axis=1)
            mixed = jnp.concatenate([v[q * 24 : (q + 1) * 24] for v in blocks], axis=0)
            modes = jnp.dot(
                leg[:, :192], mixed.astype(BF16), preferred_element_type=F32
            ).astype(BF16)
            at = pl.multiple_of((m * 2 + q) * 16, 16)
            for x in range(4):
                for g in range(8):
                    out_ref[x * 8 + g, pl.ds(at, 16), :] = modes[x * 16 : (x + 1) * 16]


def final_kernel(modes_ref, table_ref, early_ref, late_ref, field_ref, out_ref, rows_ref):
    rows, channels, cols = field_ref.shape
    for g in range(8):
        total = modes_ref[g].astype(F32)
        for x in range(1, 4):
            total += modes_ref[x * 8 + g].astype(F32)
        rows_ref[g * 64 : (g + 1) * 64, :] = total
    half = first_half((MODES, LANES))
    for m in range(rows // 2):
        one = rows_ref[pl.ds(2 * m, MODES, stride=rows), :]
        two = rows_ref[pl.ds(2 * m + 1, MODES, stride=rows), :]
        re = jnp.where(half, one, pltpu.roll(two, 64, 1))
        im = jnp.where(half, pltpu.roll(one, 64, 1), two)
        spectral = lax.dot_general(
            jnp.concatenate([re, im], axis=0).astype(BF16),
            table_ref[...],
            (((0,), (0,)), ((), ())),
            preferred_element_type=F32,
        ).astype(BF16)
        for u in range(2):
            i = 2 * m + u
            if EARLY[0] <= i < EARLY[1]:
                disco_out = early_ref[i - EARLY[0]]
            else:
                disco_out = late_ref[i if i < EARLY[0] else i - EARLY[1] + EARLY[0]]
            v = spectral[u * 64 : (u + 1) * 64].astype(F32) + disco_out
            inner = math.sqrt(2.0 / math.pi) * (v + 0.044715 * (v * v * v))
            act = 0.5 * v * (1.0 + jnp.tanh(inner))
            out_ref[2 * m + u] = (field_ref[2 * m + u].astype(F32) + act).astype(BF16)


def call(kernel, out, *args, scratch=(), flops=10**7, smem=0):
    nbytes = sum(a.size * a.dtype.itemsize for a in args)
    vmem = pl.BlockSpec(memory_space=pltpu.VMEM)
    scalar = pl.BlockSpec(memory_space=pltpu.SMEM)
    return pl.pallas_call(
        kernel,
        out_shape=out,
        in_specs=[scalar] * smem + [vmem] * (len(args) - smem),
        out_specs=jax.tree.map(lambda _: vmem, out),
        scratch_shapes=scratch,
        compiler_params=pltpu.CompilerParams(vmem_limit_bytes=16 * 2**20),
        cost_estimate=pl.CostEstimate(flops=flops, bytes_accessed=nbytes, transcendentals=0),
    )(*args)


def struct(dtype, *shape):
    return jax.ShapeDtypeStruct(shape, dtype)


def halves(row):
    v = row.astype(F32)
    blank = jnp.zeros((v.shape[0], 2 * LANES - v.shape[1]), F32)
    return v[:, :LANES], jnp.concatenate([v[:, LANES:], blank], axis=1)


def edges_kernel(core_ref, field_ref, near_ref, far_ref):
    rows, channels, cols = field_ref.shape
    lane = lax.broadcasted_iota(jnp.int32, (channels, LANES), 1)
    first = core_ref[0] == 0
    for g in range(3):
        head = jnp.zeros((channels, LANES), F32)
        tail = jnp.zeros((channels, LANES), F32)
        for m in range(min(6, rows - 6 * g)):
            low, high = halves(field_ref[g * 6 + m])
            inside = (lane >= HMAX * m) & (lane < HMAX * (m + 1))
            low = pltpu.roll(low, HMAX * m, 1) if m else low
            high = pltpu.roll(high, (HMAX * m - (cols - HMAX - LANES)) % LANES, 1)
            head = jnp.where(inside, low, head)
            tail = jnp.where(inside, high, tail)
        near_ref[g] = jnp.where(first, tail, head).astype(BF16)
        far_ref[g] = jnp.where(first, head, tail).astype(BF16)


def widened(row, left, right, m):
    cols = row.shape[1]
    edge = HMAX + cols - LANES
    lane = lax.broadcasted_iota(jnp.int32, left.shape, 1)
    low, high = (pltpu.roll(v, HMAX, 1) for v in halves(row))
    before = pltpu.roll(left, (-HMAX * m) % LANES, 1) if m else left
    after = pltpu.roll(right, (edge - HMAX * m) % LANES, 1)
    one = jnp.where(lane < HMAX, before, low)
    two = jnp.where(lane < HMAX, low, high)
    return one, jnp.where(lane < edge, two, jnp.where(lane < edge + HMAX, after, 0.0))


def sides(core_ref, near, far):
    near, far = near.astype(F32), far.astype(F32)
    first = core_ref[0] == 0
    return jnp.where(first, far, near), jnp.where(first, near, far)


def rows_kernel(core_ref, even_ref, field_ref, near_ref, far_ref, one_ref, two_ref):
    rows = field_ref.shape[0]
    ends = []
    for r in (0, rows - 1):
        left, right = sides(core_ref, near_ref[r // 6], far_ref[r // 6])
        ends.append(jnp.concatenate(widened(field_ref[r], left, right, r % 6), axis=1))
    even = even_ref[0] == 1
    one_ref[0] = jnp.where(even, ends[1], ends[0]).astype(BF16)
    two_ref[0] = jnp.where(even, ends[0], ends[1]).astype(BF16)


def toeplitz_kernel(
    spans, core_ref, even_ref, field_ref, near_ref, far_ref, one_ref, two_ref, base_ref, weight_ref,
    out_ref, ext_ref, rest_ref, band_ref,
):
    rows, channels, cols = field_ref.shape
    lane = lax.broadcasted_iota(jnp.int32, (channels, LANES), 1)
    wanted = [i for first, last in spans for i in range(first, last)]
    for r in range(rows + 2):
        if not any(i in wanted for i in (r - 2, r - 1, r)):
            continue
        if r in (0, rows + 1):
            a, b = (one_ref, two_ref) if r else (two_ref, one_ref)
            row = jnp.where(even_ref[0] == 1, a[0].astype(F32), b[0].astype(F32))
            one, two = row[:, :LANES], row[:, LANES:]
        else:
            g, m = divmod(r - 1, 6)
            left, right = sides(core_ref, near_ref[g], far_ref[g])
            one, two = widened(field_ref[r - 1], left, right, m)
        ext_ref[r, :, :LANES] = one.astype(BF16)
        ext_ref[r, :, LANES:] = two.astype(BF16)
        for a in range(3):
            i = r - a
            if i in wanted:
                part = pltpu.roll(two, 2 * HMAX * a, 1) if a else two
                inside = (lane >= 2 * HMAX * a) & (lane < 2 * HMAX * (a + 1))
                rest_ref[i] = jnp.where(inside, part, rest_ref[i] if a else 0.0)

    r = lax.broadcasted_iota(jnp.int32, (LANES, LANES), 0)
    s = lax.broadcasted_iota(jnp.int32, (LANES, LANES), 1)

    def one_row(row, at):
        for k in range(BASES):
            cols_k = slice(k * LANES, (k + 1) * LANES)
            spill = []
            for a in range(3):
                line = base_ref[row, k * 3 + a : k * 3 + a + 1, :]
                circ = pltpu.roll(
                    jnp.broadcast_to(line, (LANES, LANES)), 0, 1, stride=1, stride_axis=0
                )
                band_ref[a * LANES : (a + 1) * LANES, cols_k] = jnp.where(s <= r, circ, 0.0).astype(
                    BF16
                )
                spill.append(jnp.where(s > r, circ, 0.0)[: 2 * HMAX])
            spill.append(jnp.zeros((LANES - 6 * HMAX, LANES), F32))
            band_ref[3 * LANES :, cols_k] = jnp.concatenate(spill, axis=0).astype(BF16)
        lines = [ext_ref[row + a] for a in range(3)]
        upper = [v[:, :LANES] for v in lines] + [rest_ref[row].astype(BF16)]
        lower = [v[:, LANES:] for v in lines] + [jnp.zeros((channels, LANES), BF16)]
        lhs = jnp.concatenate(
            [jnp.concatenate(upper, axis=1), jnp.concatenate(lower, axis=1)], axis=0
        )
        sums = jnp.dot(lhs, band_ref[...], preferred_element_type=F32).astype(BF16)
        stacked = jnp.concatenate(
            [
                jnp.concatenate(
                    [
                        sums[u * channels : (u + 1) * channels, k * LANES : (k + 1) * LANES]
                        for u in range(2)
                    ],
                    axis=1,
                )
                for k in range(BASES)
            ],
            axis=0,
        )
        mixed = jnp.dot(weight_ref[...], stacked, preferred_element_type=F32)
        out_ref[at] = mixed[:, :cols]

    done = 0
    for first, last in spans:
        pl.loop(first, last)(lambda row, shift=done - first: one_row(row, row + shift))
        done += last - first


def early_kernel(core_ref, field_ref, near_ref, far_ref, base_ref, weight_ref, *refs):
    toeplitz_kernel(
        (EARLY,), core_ref, None, field_ref, near_ref, far_ref, None, None, base_ref, weight_ref, *refs
    )


def late_kernel(*refs):
    toeplitz_kernel(((0, EARLY[0]), (EARLY[1], 16)), *refs)


def lat_rows_of(field, scalars, near, far):
    row = struct(BF16, 1, field.shape[1], 2 * LANES)
    one, two = call(
        rows_kernel, (row, row), *scalars, field, near, far, smem=2, flops=2 * 10**10
    )
    lat = ("zl", "x")
    one, two, far = lax.optimization_barrier((one, two, far))
    one = lax.ppermute(one, lat, [(i, i ^ 1) for i in range(32)])
    two = lax.ppermute(two, lat, [(i, i + 1 if i % 2 else i - 1) for i in range(1, 31)])
    return far, one, two


def taps_of(channels, disco_reach, disco_taps, disco_weight):
    lat_rows = disco_taps.shape[0]
    offsets = jnp.abs(jnp.arange(TAPS, dtype=jnp.int32) - HMAX)
    within = offsets[None, :] <= disco_reach[:, None]
    coef = jnp.where(
        within[:, None, :], disco_taps.reshape(lat_rows, BASES * 3, TAPS), 0.0
    )
    base = jnp.concatenate(
        [
            coef[:, :, :1],
            jnp.zeros((lat_rows, BASES * 3, LANES - TAPS), F32),
            coef[:, :, :0:-1],
        ],
        axis=2,
    )
    weight = disco_weight.transpose(2, 0, 1).reshape(channels, BASES * channels)
    return base, weight


def disco(kernel, count, field, scalars, around, base, weight):
    lat_rows, channels, lon_cols = field.shape
    return call(
        kernel,
        struct(F32, count, channels, lon_cols),
        *scalars,
        field,
        *around,
        base,
        weight,
        smem=len(scalars),
        flops=2 * count * 128 * 512 * 512,
        scratch=[
            pltpu.VMEM((lat_rows + 2, channels, 2 * LANES), BF16),
            pltpu.VMEM((lat_rows, channels, LANES), F32),
            pltpu.VMEM((4 * LANES, BASES * LANES), BF16),
        ],
    )


def exchange(cells, axes):
    return lax.all_to_all(cells, axes, split_axis=0, concat_axis=0, tiled=True)


def line_exchange(cells):
    groups = [
        [zl * 16 + member(pair, m) for m in range(2) for zl in range(8)] for pair in range(8)
    ]
    return lax.all_to_all(
        cells, ("zl", *LON), split_axis=0, concat_axis=0, tiled=True, axis_index_groups=groups
    )


def per_device(grid_field, disco_reach, disco_taps, disco_weight, legendre, mixing):
    lat_rows, lon_cols, channels = grid_field.shape
    wide = 2 * channels
    own = mixing.shape[0]
    place = lax.axis_index(LON)
    field = grid_field.transpose(0, 2, 1)
    forward = table(lon_cols, 1.0 / math.sqrt(NLON), lambda sector: np.arange(MODES))
    inverse = table(lon_cols, 1.0 / math.sqrt(MODES), lambda sector: orders_at(sector // 2 % 2))
    forward = lax.dynamic_index_in_dim(jnp.asarray(forward), place, 0, keepdims=False)
    inverse = lax.dynamic_index_in_dim(jnp.asarray(inverse), place, 0, keepdims=False)
    spread = [pltpu.VMEM((MODES * lat_rows, wide), F32)]

    core = lax.axis_index("core").reshape(1)
    even = (1 - lax.axis_index("x") % 2).reshape(1)
    waves = call(
        forward_kernel, struct(BF16, 16, 2 * lat_rows, wide), field, forward, scratch=spread
    )
    waves = exchange(waves, LON)
    packed = struct(BF16, 3, channels, LANES)
    near, far = call(edges_kernel, (packed, packed), core, field, smem=1)
    near = lax.ppermute(near, LON, [(i, i ^ 1) for i in range(16)])
    base, taps_weight = taps_of(channels, disco_reach, disco_taps, disco_weight)
    weight = jnp.concatenate([mixing[:, 0], mixing[:, 1]], axis=2)
    legs = call(
        legs_kernel,
        struct(BF16, 4, 2 * lat_rows, 256),
        (place * 2).astype(jnp.int32).reshape(1),
        legendre,
        jnp.asarray(degree_order()),
        smem=1,
        scratch=[
            pltpu.VMEM((2 * lat_rows, 768), F32),
            pltpu.VMEM((2, 8 * lat_rows, LANES), F32),
        ],
    )
    waves, near, far, legs, inverse, base, taps_weight = lax.optimization_barrier(
        (waves, near, far, legs, inverse, base, taps_weight)
    )
    message = call(spectra_kernel, struct(BF16, 4, 2 * lat_rows, 384), waves, legs)
    message = exchange(message, ("x",))
    coeffs, leg, mine = call(
        analysis_kernel,
        (
            struct(BF16, 8, 2 * own, wide),
            struct(BF16, 2, 4 * lat_rows, 256),
            struct(BF16, 7, 4 * lat_rows, LANES),
        ),
        message,
        far,
    )
    coeffs = exchange(coeffs, ("zl",))
    swap = [(i, member(pair_of(i), i % 2)) for i in range(16)]
    far = lax.ppermute(mine, LON, swap)
    far, one, two = lat_rows_of(field, (core, even), near, far)
    mixed = call(mixing_kernel, struct(BF16, 16, 2 * own, wide), coeffs, weight)
    mixed = line_exchange(mixed)
    early = disco(
        early_kernel, EARLY[1] - EARLY[0], field, (core,), (near, far), base, taps_weight
    )
    mixed, one, two, early = lax.optimization_barrier((mixed, one, two, early))
    modes = call(
        synthesis_kernel,
        struct(BF16, 32, 4 * lat_rows, wide),
        1 - core,
        mixed,
        leg,
        far,
        smem=1,
    )
    modes = exchange(modes, ("x", "y", "core"))
    late = disco(
        late_kernel,
        lat_rows - EARLY[1] + EARLY[0],
        field,
        (core, even),
        (near, far, one, two),
        base,
        taps_weight,
    )
    out = call(
        final_kernel,
        struct(BF16, lat_rows, channels, lon_cols),
        modes,
        inverse,
        early,
        late,
        field,
        scratch=spread,
    )
    return out.transpose(0, 2, 1)


def solution(mesh):
    fine = Mesh(mesh.devices.reshape(8, 4, 4, 2, 2), ("zl", "x", "y", "zh", "core"))
    lat, lon = ("zl", "x"), LON
    in_specs = (
        P(lat, lon, None),
        P(lat),
        P(lat, None),
        P(),
        P(lat, lon, None),
        P(lat, None, None, None),
    )
    return jax.shard_map(
        per_device, mesh=fine, in_specs=in_specs, out_specs=P(lat, lon, None), check_vma=False
    )
```

```python
import math

import jax
import jax.numpy as jnp
import numpy as np
from jax import lax
from jax.experimental import pallas as pl
from jax.experimental.pallas import tpu as pltpu
from jax.sharding import Mesh
from jax.sharding import PartitionSpec as P

NLON = 2880
MODES = 32
HMAX = 20
TAPS = 2 * HMAX + 1
BASES = 4
LANES = 128
BF16 = jnp.bfloat16
F32 = jnp.float32
LON = ("y", "zh", "core")
EARLY = (1, 4)


def pair_of(sector):
    return (sector + 15) % 16 // 2


def member(pair, m):
    return (2 * pair + 1 + m) % 16


def orders_at(zh):
    out = []
    for group in range(8):
        pair = pair_of(group // 2 * 4 + zh * 2 + group % 2)
        out += [member(pair, m) * 2 + odd for m in range(2) for odd in range(2)]
    return np.array(out)


def table(lon_cols, scale, orders_of):
    sectors = []
    for sector in range(NLON // lon_cols):
        columns = sector * lon_cols + np.arange(lon_cols)
        residues = (orders_of(sector)[:, None] * columns[None, :]) % NLON
        phases = residues.astype(np.float32) * np.float32(2.0 * math.pi / NLON)
        sectors.append(np.concatenate([np.cos(phases), -np.sin(phases)], axis=0))
    return (np.stack(sectors).astype(np.float32) * np.float32(scale)).astype(BF16)


def degree_order():
    out = np.zeros((768, 256), np.float32)
    for o in range(192):
        out[o // 24 * 96 + o % 24, o] = 1.0
    return out.astype(BF16)


def first_half(shape):
    return lax.broadcasted_iota(jnp.int32, shape, len(shape) - 1) < 64


def forward_kernel(field_ref, table_ref, out_ref, rows_ref):
    rows = field_ref.shape[0]
    field = field_ref[...].reshape(rows * 64, field_ref.shape[2])
    waves = lax.dot_general(
        table_ref[...], field, (((1,), (1,)), ((), ())), preferred_element_type=F32
    )
    half = first_half((MODES, LANES))
    for m in range(rows // 2):
        re = waves[:MODES, m * LANES : (m + 1) * LANES]
        im = waves[MODES:, m * LANES : (m + 1) * LANES]
        rows_ref[pl.ds(2 * m, MODES, stride=rows), :] = jnp.where(half, re, pltpu.roll(im, 64, 1))
        rows_ref[pl.ds(2 * m + 1, MODES, stride=rows), :] = jnp.where(
            half, pltpu.roll(re, 64, 1), im
        )
    out_ref[...] = rows_ref[...].astype(BF16).reshape(out_ref.shape)


def spectra_kernel(waves_ref, legs_ref, out_ref):
    total = waves_ref[0].astype(F32)
    for n in range(1, waves_ref.shape[0]):
        total += waves_ref[n].astype(F32)
    spectra = total.astype(BF16)
    for x in range(4):
        out_ref[x, :, :LANES] = spectra
        out_ref[x, :, LANES:] = legs_ref[x]


def legs_kernel(orders_ref, leg_ref, pick_ref, out_ref, rows_ref, lines_ref):
    rows = leg_ref.shape[0]
    for i in range(rows):
        rows_ref[2 * i : 2 * i + 2, :] = leg_ref[i].astype(F32)
    row = lax.broadcasted_iota(jnp.int32, (2 * rows, LANES), 0)
    degree = lax.broadcasted_iota(jnp.int32, (2 * rows, LANES), 1)
    low = jnp.where(degree >= orders_ref[0] + row % 2, rows_ref[:, :LANES], 0.0)
    lines = jnp.concatenate([low, rows_ref[:, LANES:]], axis=1)
    turned = [lines] + [pltpu.roll(lines, 768 - 24 * x, 1) for x in range(1, 4)]
    turned = jnp.concatenate(turned, axis=0).astype(BF16)
    picked = jnp.dot(turned, pick_ref[...], preferred_element_type=F32)
    for t in range(2):
        lines_ref[t] = picked[:, t * LANES : (t + 1) * LANES]
    for q in range(2):
        for x in range(4):
            for t in range(2):
                v = lines_ref[t, pl.ds(x * 2 * rows + q, rows, stride=2), :]
                out_ref[x, q * rows : (q + 1) * rows, t * LANES : (t + 1) * LANES] = v.astype(BF16)


def analysis_kernel(got_ref, far_ref, coeff_ref, leg_ref, pack_ref):
    parts, highs = [], []
    for q in range(2):
        both = jnp.concatenate([got_ref[x, q * 16 : (q + 1) * 16, :] for x in range(4)], axis=0)
        leg_ref[q] = both[:, LANES:]
        pack_ref[3 + q] = both[:, LANES : 2 * LANES]
        highs.append(both[:, 2 * LANES :].astype(F32))
        parts.append(
            lax.dot_general(
                both[:, LANES:],
                both[:, :LANES],
                (((0,), (0,)), ((), ())),
                preferred_element_type=F32,
            )
        )
    for n in range(8):
        rows = jnp.concatenate([p[n * 24 : (n + 1) * 24] for p in parts], axis=0)
        coeff_ref[n] = rows.astype(BF16)
    for n in range(3):
        pack_ref[n] = far_ref[n]
    high = jnp.where(first_half(highs[0].shape), highs[0], pltpu.roll(highs[1], 64, 1))
    pack_ref[5] = high.astype(BF16)


def mixing_kernel(coeff_ref, weight_ref, out_ref):
    total = coeff_ref[0].astype(F32)
    for n in range(1, coeff_ref.shape[0]):
        total += coeff_ref[n].astype(F32)
    lhs = jnp.concatenate([total[:, :64], total[:, 64:]], axis=0).astype(BF16)
    degree = lax.broadcasted_iota(jnp.int32, (96, LANES), 0) % 24
    acc = jnp.zeros((96, LANES), F32)
    for l in range(24):
        acc = jnp.where(
            degree == l, jnp.dot(lhs, weight_ref[l], preferred_element_type=F32), acc
        )
    turned = pltpu.roll(acc[48:], 64, 1)
    mixed = acc[:48] + jnp.where(first_half((48, LANES)), -turned, turned)
    mixed = mixed.astype(BF16)
    for n in range(out_ref.shape[0]):
        out_ref[n] = mixed


def synthesis_kernel(mate_ref, mixed_ref, own_ref, other_ref, out_ref):
    for side in range(2):
        m = mate_ref[0] if side == 0 else 1 - mate_ref[0]
        blocks = [mixed_ref[m * 8 + n].astype(F32) for n in range(8)]
        for q in range(2):
            if side == 0:
                leg = own_ref[q]
            else:
                high = other_ref[5].astype(F32)
                high = pltpu.roll(high, 64, 1) if q else high
                leg = jnp.concatenate([other_ref[3 + q], high.astype(BF16)], axis=1)
            mixed = jnp.concatenate([v[q * 24 : (q + 1) * 24] for v in blocks], axis=0)
            modes = jnp.dot(
                leg[:, :192], mixed.astype(BF16), preferred_element_type=F32
            ).astype(BF16)
            at = pl.multiple_of((m * 2 + q) * 16, 16)
            for x in range(4):
                for g in range(8):
                    out_ref[x * 8 + g, pl.ds(at, 16), :] = modes[x * 16 : (x + 1) * 16]


def final_kernel(modes_ref, table_ref, early_ref, late_ref, field_ref, out_ref, rows_ref):
    rows, channels, cols = field_ref.shape
    for g in range(8):
        total = modes_ref[g].astype(F32)
        for x in range(1, 4):
            total += modes_ref[x * 8 + g].astype(F32)
        rows_ref[g * 64 : (g + 1) * 64, :] = total
    half = first_half((MODES, LANES))
    for m in range(rows // 2):
        one = rows_ref[pl.ds(2 * m, MODES, stride=rows), :]
        two = rows_ref[pl.ds(2 * m + 1, MODES, stride=rows), :]
        re = jnp.where(half, one, pltpu.roll(two, 64, 1))
        im = jnp.where(half, pltpu.roll(one, 64, 1), two)
        spectral = lax.dot_general(
            jnp.concatenate([re, im], axis=0).astype(BF16),
            table_ref[...],
            (((0,), (0,)), ((), ())),
            preferred_element_type=F32,
        ).astype(BF16)
        for u in range(2):
            i = 2 * m + u
            if EARLY[0] <= i < EARLY[1]:
                disco_out = early_ref[i - EARLY[0]]
            else:
                disco_out = late_ref[i if i < EARLY[0] else i - EARLY[1] + EARLY[0]]
            v = spectral[u * 64 : (u + 1) * 64].astype(F32) + disco_out
            inner = math.sqrt(2.0 / math.pi) * (v + 0.044715 * (v * v * v))
            act = 0.5 * v * (1.0 + jnp.tanh(inner))
            out_ref[2 * m + u] = (field_ref[2 * m + u].astype(F32) + act).astype(BF16)


def call(kernel, out, *args, scratch=(), flops=10**7, smem=0):
    nbytes = sum(a.size * a.dtype.itemsize for a in args)
    vmem = pl.BlockSpec(memory_space=pltpu.VMEM)
    scalar = pl.BlockSpec(memory_space=pltpu.SMEM)
    return pl.pallas_call(
        kernel,
        out_shape=out,
        in_specs=[scalar] * smem + [vmem] * (len(args) - smem),
        out_specs=jax.tree.map(lambda _: vmem, out),
        scratch_shapes=scratch,
        compiler_params=pltpu.CompilerParams(vmem_limit_bytes=16 * 2**20),
        cost_estimate=pl.CostEstimate(flops=flops, bytes_accessed=nbytes, transcendentals=0),
    )(*args)


def struct(dtype, *shape):
    return jax.ShapeDtypeStruct(shape, dtype)


def halves(row):
    v = row.astype(F32)
    blank = jnp.zeros((v.shape[0], 2 * LANES - v.shape[1]), F32)
    return v[:, :LANES], jnp.concatenate([v[:, LANES:], blank], axis=1)


def edges_kernel(core_ref, field_ref, near_ref, far_ref):
    rows, channels, cols = field_ref.shape
    lane = lax.broadcasted_iota(jnp.int32, (channels, LANES), 1)
    first = core_ref[0] == 0
    for g in range(3):
        head = jnp.zeros((channels, LANES), F32)
        tail = jnp.zeros((channels, LANES), F32)
        for m in range(min(6, rows - 6 * g)):
            low, high = halves(field_ref[g * 6 + m])
            inside = (lane >= HMAX * m) & (lane < HMAX * (m + 1))
            low = pltpu.roll(low, HMAX * m, 1) if m else low
            high = pltpu.roll(high, (HMAX * m - (cols - HMAX - LANES)) % LANES, 1)
            head = jnp.where(inside, low, head)
            tail = jnp.where(inside, high, tail)
        near_ref[g] = jnp.where(first, tail, head).astype(BF16)
        far_ref[g] = jnp.where(first, head, tail).astype(BF16)


def widened(row, left, right, m):
    cols = row.shape[1]
    edge = HMAX + cols - LANES
    lane = lax.broadcasted_iota(jnp.int32, left.shape, 1)
    low, high = (pltpu.roll(v, HMAX, 1) for v in halves(row))
    before = pltpu.roll(left, (-HMAX * m) % LANES, 1) if m else left
    after = pltpu.roll(right, (edge - HMAX * m) % LANES, 1)
    one = jnp.where(lane < HMAX, before, low)
    two = jnp.where(lane < HMAX, low, high)
    return one, jnp.where(lane < edge, two, jnp.where(lane < edge + HMAX, after, 0.0))


def sides(core_ref, near, far):
    near, far = near.astype(F32), far.astype(F32)
    first = core_ref[0] == 0
    return jnp.where(first, far, near), jnp.where(first, near, far)


def rows_kernel(core_ref, even_ref, field_ref, near_ref, far_ref, one_ref, two_ref):
    rows = field_ref.shape[0]
    ends = []
    for r in (0, rows - 1):
        left, right = sides(core_ref, near_ref[r // 6], far_ref[r // 6])
        ends.append(jnp.concatenate(widened(field_ref[r], left, right, r % 6), axis=1))
    even = even_ref[0] == 1
    one_ref[0] = jnp.where(even, ends[1], ends[0]).astype(BF16)
    two_ref[0] = jnp.where(even, ends[0], ends[1]).astype(BF16)


def toeplitz_kernel(
    spans, core_ref, even_ref, field_ref, near_ref, far_ref, one_ref, two_ref, base_ref, weight_ref,
    out_ref, ext_ref, rest_ref, band_ref,
):
    rows, channels, cols = field_ref.shape
    lane = lax.broadcasted_iota(jnp.int32, (channels, LANES), 1)
    wanted = [i for first, last in spans for i in range(first, last)]
    for r in range(rows + 2):
        if not any(i in wanted for i in (r - 2, r - 1, r)):
            continue
        if r in (0, rows + 1):
            a, b = (one_ref, two_ref) if r else (two_ref, one_ref)
            row = jnp.where(even_ref[0] == 1, a[0].astype(F32), b[0].astype(F32))
            one, two = row[:, :LANES], row[:, LANES:]
        else:
            g, m = divmod(r - 1, 6)
            left, right = sides(core_ref, near_ref[g], far_ref[g])
            one, two = widened(field_ref[r - 1], left, right, m)
        ext_ref[r, :, :LANES] = one.astype(BF16)
        ext_ref[r, :, LANES:] = two.astype(BF16)
        for a in range(3):
            i = r - a
            if i in wanted:
                part = pltpu.roll(two, 2 * HMAX * a, 1) if a else two
                inside = (lane >= 2 * HMAX * a) & (lane < 2 * HMAX * (a + 1))
                rest_ref[i] = jnp.where(inside, part, rest_ref[i] if a else 0.0)

    r = lax.broadcasted_iota(jnp.int32, (LANES, LANES), 0)
    s = lax.broadcasted_iota(jnp.int32, (LANES, LANES), 1)

    def one_row(row, at):
        for k in range(BASES):
            cols_k = slice(k * LANES, (k + 1) * LANES)
            spill = []
            for a in range(3):
                line = base_ref[row, k * 3 + a : k * 3 + a + 1, :]
                circ = pltpu.roll(
                    jnp.broadcast_to(line, (LANES, LANES)), 0, 1, stride=1, stride_axis=0
                )
                band_ref[a * LANES : (a + 1) * LANES, cols_k] = jnp.where(s <= r, circ, 0.0).astype(
                    BF16
                )
                spill.append(jnp.where(s > r, circ, 0.0)[: 2 * HMAX])
            spill.append(jnp.zeros((LANES - 6 * HMAX, LANES), F32))
            band_ref[3 * LANES :, cols_k] = jnp.concatenate(spill, axis=0).astype(BF16)
        lines = [ext_ref[row + a] for a in range(3)]
        upper = [v[:, :LANES] for v in lines] + [rest_ref[row].astype(BF16)]
        lower = [v[:, LANES:] for v in lines] + [jnp.zeros((channels, LANES), BF16)]
        lhs = jnp.concatenate(
            [jnp.concatenate(upper, axis=1), jnp.concatenate(lower, axis=1)], axis=0
        )
        sums = jnp.dot(lhs, band_ref[...], preferred_element_type=F32).astype(BF16)
        stacked = jnp.concatenate(
            [
                jnp.concatenate(
                    [
                        sums[u * channels : (u + 1) * channels, k * LANES : (k + 1) * LANES]
                        for u in range(2)
                    ],
                    axis=1,
                )
                for k in range(BASES)
            ],
            axis=0,
        )
        mixed = jnp.dot(weight_ref[...], stacked, preferred_element_type=F32)
        out_ref[at] = mixed[:, :cols]

    done = 0
    for first, last in spans:
        pl.loop(first, last)(lambda row, shift=done - first: one_row(row, row + shift))
        done += last - first


def early_kernel(core_ref, field_ref, near_ref, far_ref, base_ref, weight_ref, *refs):
    toeplitz_kernel(
        (EARLY,), core_ref, None, field_ref, near_ref, far_ref, None, None, base_ref, weight_ref, *refs
    )


def late_kernel(*refs):
    toeplitz_kernel(((0, EARLY[0]), (EARLY[1], 16)), *refs)


def lat_rows_of(field, scalars, near, far):
    row = struct(BF16, 1, field.shape[1], 2 * LANES)
    one, two = call(
        rows_kernel, (row, row), *scalars, field, near, far, smem=2, flops=2 * 10**10
    )
    lat = ("zl", "x")
    one, two, far = lax.optimization_barrier((one, two, far))
    one = lax.ppermute(one, lat, [(i, i ^ 1) for i in range(32)])
    two = lax.ppermute(two, lat, [(i, i + 1 if i % 2 else i - 1) for i in range(1, 31)])
    return far, one, two


def taps_of(channels, disco_reach, disco_taps, disco_weight):
    lat_rows = disco_taps.shape[0]
    offsets = jnp.abs(jnp.arange(TAPS, dtype=jnp.int32) - HMAX)
    within = offsets[None, :] <= disco_reach[:, None]
    coef = jnp.where(
        within[:, None, :], disco_taps.reshape(lat_rows, BASES * 3, TAPS), 0.0
    )
    base = jnp.concatenate(
        [
            coef[:, :, :1],
            jnp.zeros((lat_rows, BASES * 3, LANES - TAPS), F32),
            coef[:, :, :0:-1],
        ],
        axis=2,
    )
    weight = disco_weight.transpose(2, 0, 1).reshape(channels, BASES * channels)
    return base, weight


def disco(kernel, count, field, scalars, around, base, weight):
    lat_rows, channels, lon_cols = field.shape
    return call(
        kernel,
        struct(F32, count, channels, lon_cols),
        *scalars,
        field,
        *around,
        base,
        weight,
        smem=len(scalars),
        flops=2 * count * 128 * 512 * 512,
        scratch=[
            pltpu.VMEM((lat_rows + 2, channels, 2 * LANES), BF16),
            pltpu.VMEM((lat_rows, channels, LANES), F32),
            pltpu.VMEM((4 * LANES, BASES * LANES), BF16),
        ],
    )


def exchange(cells, axes):
    return lax.all_to_all(cells, axes, split_axis=0, concat_axis=0, tiled=True)


def line_exchange(cells):
    groups = [
        [zl * 16 + member(pair, m) for m in range(2) for zl in range(8)] for pair in range(8)
    ]
    return lax.all_to_all(
        cells, ("zl", *LON), split_axis=0, concat_axis=0, tiled=True, axis_index_groups=groups
    )


def per_device(grid_field, disco_reach, disco_taps, disco_weight, legendre, mixing):
    lat_rows, lon_cols, channels = grid_field.shape
    wide = 2 * channels
    own = mixing.shape[0]
    place = lax.axis_index(LON)
    field = grid_field.transpose(0, 2, 1)
    forward = table(lon_cols, 1.0 / math.sqrt(NLON), lambda sector: np.arange(MODES))
    inverse = table(lon_cols, 1.0 / math.sqrt(MODES), lambda sector: orders_at(sector // 2 % 2))
    forward = lax.dynamic_index_in_dim(jnp.asarray(forward), place, 0, keepdims=False)
    inverse = lax.dynamic_index_in_dim(jnp.asarray(inverse), place, 0, keepdims=False)
    spread = [pltpu.VMEM((MODES * lat_rows, wide), F32)]

    core = lax.axis_index("core").reshape(1)
    even = (1 - lax.axis_index("x") % 2).reshape(1)
    waves = call(
        forward_kernel, struct(BF16, 16, 2 * lat_rows, wide), field, forward, scratch=spread
    )
    waves = exchange(waves, LON)
    packed = struct(BF16, 3, channels, LANES)
    near, far = call(edges_kernel, (packed, packed), core, field, smem=1)
    near = lax.ppermute(near, LON, [(i, i ^ 1) for i in range(16)])
    base, taps_weight = taps_of(channels, disco_reach, disco_taps, disco_weight)
    weight = jnp.concatenate([mixing[:, 0], mixing[:, 1]], axis=2)
    legs = call(
        legs_kernel,
        struct(BF16, 4, 2 * lat_rows, 256),
        (place * 2).astype(jnp.int32).reshape(1),
        legendre,
        jnp.asarray(degree_order()),
        smem=1,
        scratch=[
            pltpu.VMEM((2 * lat_rows, 768), F32),
            pltpu.VMEM((2, 8 * lat_rows, LANES), F32),
        ],
    )
    waves, near, far, legs, inverse, base, taps_weight = lax.optimization_barrier(
        (waves, near, far, legs, inverse, base, taps_weight)
    )
    message = call(spectra_kernel, struct(BF16, 4, 2 * lat_rows, 384), waves, legs)
    message = exchange(message, ("x",))
    coeffs, leg, mine = call(
        analysis_kernel,
        (
            struct(BF16, 8, 2 * own, wide),
            struct(BF16, 2, 4 * lat_rows, 256),
            struct(BF16, 6, 4 * lat_rows, LANES),
        ),
        message,
        far,
    )
    coeffs = exchange(coeffs, ("zl",))
    swap = [(i, member(pair_of(i), i % 2)) for i in range(16)]
    far = lax.ppermute(mine, LON, swap)
    far, one, two = lat_rows_of(field, (core, even), near, far)
    mixed = call(mixing_kernel, struct(BF16, 16, 2 * own, wide), coeffs, weight)
    mixed = line_exchange(mixed)
    early = disco(
        early_kernel, EARLY[1] - EARLY[0], field, (core,), (near, far), base, taps_weight
    )
    mixed, one, two, early = lax.optimization_barrier((mixed, one, two, early))
    modes = call(
        synthesis_kernel,
        struct(BF16, 32, 4 * lat_rows, wide),
        1 - core,
        mixed,
        leg,
        far,
        smem=1,
    )
    modes = exchange(modes, ("x", "y", "core"))
    late = disco(
        late_kernel,
        lat_rows - EARLY[1] + EARLY[0],
        field,
        (core, even),
        (near, far, one, two),
        base,
        taps_weight,
    )
    out = call(
        final_kernel,
        struct(BF16, lat_rows, channels, lon_cols),
        modes,
        inverse,
        early,
        late,
        field,
        scratch=spread,
    )
    return out.transpose(0, 2, 1)


def solution(mesh):
    fine = Mesh(mesh.devices.reshape(8, 4, 4, 2, 2), ("zl", "x", "y", "zh", "core"))
    lat, lon = ("zl", "x"), LON
    in_specs = (
        P(lat, lon, None),
        P(lat),
        P(lat, None),
        P(),
        P(lat, lon, None),
        P(lat, None, None, None),
    )
    return jax.shard_map(
        per_device, mesh=fine, in_specs=in_specs, out_specs=P(lat, lon, None), check_vma=False
    )
```

```python
import math

import jax
import jax.numpy as jnp
import numpy as np
from jax import lax
from jax.experimental import pallas as pl
from jax.experimental.pallas import tpu as pltpu
from jax.sharding import Mesh
from jax.sharding import PartitionSpec as P

NLON = 2880
MODES = 32
HMAX = 20
TAPS = 2 * HMAX + 1
BASES = 4
LANES = 128
BF16 = jnp.bfloat16
F32 = jnp.float32
LON = ("y", "zh", "core")
EARLY = (1, 4)


def pair_of(sector):
    return (sector + 15) % 16 // 2


def member(pair, m):
    return (2 * pair + 1 + m) % 16


def orders_at(zh):
    out = []
    for group in range(8):
        pair = pair_of(group // 2 * 4 + zh * 2 + group % 2)
        out += [member(pair, m) * 2 + odd for m in range(2) for odd in range(2)]
    return np.array(out)


def table(lon_cols, scale, orders_of):
    sectors = []
    for sector in range(NLON // lon_cols):
        columns = sector * lon_cols + np.arange(lon_cols)
        residues = (orders_of(sector)[:, None] * columns[None, :]) % NLON
        phases = residues.astype(np.float32) * np.float32(2.0 * math.pi / NLON)
        sectors.append(np.concatenate([np.cos(phases), -np.sin(phases)], axis=0))
    return (np.stack(sectors).astype(np.float32) * np.float32(scale)).astype(BF16)


def degree_order():
    out = np.zeros((768, 256), np.float32)
    for o in range(192):
        out[o // 24 * 96 + o % 24, o] = 1.0
    return out.astype(BF16)


def first_half(shape):
    return lax.broadcasted_iota(jnp.int32, shape, len(shape) - 1) < 64


def forward_kernel(field_ref, table_ref, out_ref, rows_ref):
    rows = field_ref.shape[0]
    field = field_ref[...].reshape(rows * 64, field_ref.shape[2])
    waves = lax.dot_general(
        table_ref[...], field, (((1,), (1,)), ((), ())), preferred_element_type=F32
    )
    half = first_half((MODES, LANES))
    for m in range(rows // 2):
        re = waves[:MODES, m * LANES : (m + 1) * LANES]
        im = waves[MODES:, m * LANES : (m + 1) * LANES]
        rows_ref[pl.ds(2 * m, MODES, stride=rows), :] = jnp.where(half, re, pltpu.roll(im, 64, 1))
        rows_ref[pl.ds(2 * m + 1, MODES, stride=rows), :] = jnp.where(
            half, pltpu.roll(re, 64, 1), im
        )
    out_ref[...] = rows_ref[...].astype(BF16).reshape(out_ref.shape)


def spectra_kernel(waves_ref, legs_ref, out_ref):
    total = waves_ref[0].astype(F32)
    for n in range(1, waves_ref.shape[0]):
        total += waves_ref[n].astype(F32)
    spectra = total.astype(BF16)
    for x in range(4):
        out_ref[x, :, :LANES] = spectra
        out_ref[x, :, LANES:] = legs_ref[x]


def legs_kernel(orders_ref, leg_ref, pick_ref, out_ref, rows_ref, lines_ref):
    rows = leg_ref.shape[0]
    for i in range(rows):
        rows_ref[2 * i : 2 * i + 2, :] = leg_ref[i].astype(F32)
    row = lax.broadcasted_iota(jnp.int32, (2 * rows, LANES), 0)
    degree = lax.broadcasted_iota(jnp.int32, (2 * rows, LANES), 1)
    low = jnp.where(degree >= orders_ref[0] + row % 2, rows_ref[:, :LANES], 0.0)
    lines = jnp.concatenate([low, rows_ref[:, LANES:]], axis=1)
    turned = [lines] + [pltpu.roll(lines, 768 - 24 * x, 1) for x in range(1, 4)]
    turned = jnp.concatenate(turned, axis=0).astype(BF16)
    picked = jnp.dot(turned, pick_ref[...], preferred_element_type=F32)
    for t in range(2):
        lines_ref[t] = picked[:, t * LANES : (t + 1) * LANES]
    for q in range(2):
        for x in range(4):
            for t in range(2):
                v = lines_ref[t, pl.ds(x * 2 * rows + q, rows, stride=2), :]
                out_ref[x, q * rows : (q + 1) * rows, t * LANES : (t + 1) * LANES] = v.astype(BF16)


def analysis_kernel(got_ref, far_ref, coeff_ref, leg_ref, pack_ref):
    parts, highs = [], []
    for q in range(2):
        both = jnp.concatenate([got_ref[x, q * 16 : (q + 1) * 16, :] for x in range(4)], axis=0)
        leg_ref[q] = both[:, LANES:]
        pack_ref[3 + q] = both[:, LANES : 2 * LANES]
        highs.append(both[:, 2 * LANES :].astype(F32))
        parts.append(
            lax.dot_general(
                both[:, LANES:],
                both[:, :LANES],
                (((0,), (0,)), ((), ())),
                preferred_element_type=F32,
            )
        )
    for n in range(8):
        rows = jnp.concatenate([p[n * 24 : (n + 1) * 24] for p in parts], axis=0)
        coeff_ref[n] = rows.astype(BF16)
    for n in range(3):
        pack_ref[n] = far_ref[n]
    high = jnp.where(first_half(highs[0].shape), highs[0], pltpu.roll(highs[1], 64, 1))
    pack_ref[5] = high.astype(BF16)


def mixing_kernel(coeff_ref, weight_ref, out_ref):
    total = coeff_ref[0].astype(F32)
    for n in range(1, coeff_ref.shape[0]):
        total += coeff_ref[n].astype(F32)
    lhs = jnp.concatenate([total[:, :64], total[:, 64:]], axis=0).astype(BF16)
    degree = lax.broadcasted_iota(jnp.int32, (96, LANES), 0) % 24
    acc = jnp.zeros((96, LANES), F32)
    for l in range(24):
        acc = jnp.where(
            degree == l, jnp.dot(lhs, weight_ref[l], preferred_element_type=F32), acc
        )
    turned = pltpu.roll(acc[48:], 64, 1)
    mixed = acc[:48] + jnp.where(first_half((48, LANES)), -turned, turned)
    mixed = mixed.astype(BF16)
    for n in range(out_ref.shape[0]):
        out_ref[n] = mixed


def synthesis_kernel(mate_ref, mixed_ref, own_ref, other_ref, out_ref):
    for side in range(2):
        m = mate_ref[0] if side == 0 else 1 - mate_ref[0]
        blocks = [mixed_ref[m * 8 + n].astype(F32) for n in range(8)]
        for q in range(2):
            if side == 0:
                leg = own_ref[q]
            else:
                high = other_ref[5].astype(F32)
                high = pltpu.roll(high, 64, 1) if q else high
                leg = jnp.concatenate([other_ref[3 + q], high.astype(BF16)], axis=1)
            mixed = jnp.concatenate([v[q * 24 : (q + 1) * 24] for v in blocks], axis=0)
            modes = jnp.dot(
                leg[:, :192], mixed.astype(BF16), preferred_element_type=F32
            ).astype(BF16)
            at = pl.multiple_of((m * 2 + q) * 16, 16)
            for x in range(4):
                for g in range(8):
                    out_ref[x * 8 + g, pl.ds(at, 16), :] = modes[x * 16 : (x + 1) * 16]


def final_kernel(modes_ref, table_ref, early_ref, late_ref, field_ref, out_ref, rows_ref):
    rows, channels, cols = field_ref.shape
    for g in range(8):
        total = modes_ref[g].astype(F32)
        for x in range(1, 4):
            total += modes_ref[x * 8 + g].astype(F32)
        rows_ref[g * 64 : (g + 1) * 64, :] = total
    half = first_half((MODES, LANES))
    for m in range(rows // 2):
        one = rows_ref[pl.ds(2 * m, MODES, stride=rows), :]
        two = rows_ref[pl.ds(2 * m + 1, MODES, stride=rows), :]
        re = jnp.where(half, one, pltpu.roll(two, 64, 1))
        im = jnp.where(half, pltpu.roll(one, 64, 1), two)
        spectral = lax.dot_general(
            jnp.concatenate([re, im], axis=0).astype(BF16),
            table_ref[...],
            (((0,), (0,)), ((), ())),
            preferred_element_type=F32,
        ).astype(BF16)
        for u in range(2):
            i = 2 * m + u
            if EARLY[0] <= i < EARLY[1]:
                disco_out = early_ref[i - EARLY[0]]
            else:
                disco_out = late_ref[i if i < EARLY[0] else i - EARLY[1] + EARLY[0]]
            v = spectral[u * 64 : (u + 1) * 64].astype(F32) + disco_out
            inner = math.sqrt(2.0 / math.pi) * (v + 0.044715 * (v * v * v))
            act = 0.5 * v * (1.0 + jnp.tanh(inner))
            out_ref[2 * m + u] = (field_ref[2 * m + u].astype(F32) + act).astype(BF16)


def call(kernel, out, *args, scratch=(), flops=10**7, smem=0):
    nbytes = sum(a.size * a.dtype.itemsize for a in args)
    vmem = pl.BlockSpec(memory_space=pltpu.VMEM)
    scalar = pl.BlockSpec(memory_space=pltpu.SMEM)
    return pl.pallas_call(
        kernel,
        out_shape=out,
        in_specs=[scalar] * smem + [vmem] * (len(args) - smem),
        out_specs=jax.tree.map(lambda _: vmem, out),
        scratch_shapes=scratch,
        compiler_params=pltpu.CompilerParams(vmem_limit_bytes=16 * 2**20),
        cost_estimate=pl.CostEstimate(flops=flops, bytes_accessed=nbytes, transcendentals=0),
    )(*args)


def struct(dtype, *shape):
    return jax.ShapeDtypeStruct(shape, dtype)


def halves(row):
    v = row.astype(F32)
    blank = jnp.zeros((v.shape[0], 2 * LANES - v.shape[1]), F32)
    return v[:, :LANES], jnp.concatenate([v[:, LANES:], blank], axis=1)


def edges_kernel(core_ref, field_ref, near_ref, far_ref):
    rows, channels, cols = field_ref.shape
    lane = lax.broadcasted_iota(jnp.int32, (channels, LANES), 1)
    first = core_ref[0] == 0
    for g in range(3):
        head = jnp.zeros((channels, LANES), F32)
        tail = jnp.zeros((channels, LANES), F32)
        for m in range(min(6, rows - 6 * g)):
            low, high = halves(field_ref[g * 6 + m])
            inside = (lane >= HMAX * m) & (lane < HMAX * (m + 1))
            low = pltpu.roll(low, HMAX * m, 1) if m else low
            high = pltpu.roll(high, (HMAX * m - (cols - HMAX - LANES)) % LANES, 1)
            head = jnp.where(inside, low, head)
            tail = jnp.where(inside, high, tail)
        near_ref[g] = jnp.where(first, tail, head).astype(BF16)
        far_ref[g] = jnp.where(first, head, tail).astype(BF16)


def widened(row, left, right, m):
    cols = row.shape[1]
    edge = HMAX + cols - LANES
    lane = lax.broadcasted_iota(jnp.int32, left.shape, 1)
    low, high = (pltpu.roll(v, HMAX, 1) for v in halves(row))
    before = pltpu.roll(left, (-HMAX * m) % LANES, 1) if m else left
    after = pltpu.roll(right, (edge - HMAX * m) % LANES, 1)
    one = jnp.where(lane < HMAX, before, low)
    two = jnp.where(lane < HMAX, low, high)
    return one, jnp.where(lane < edge, two, jnp.where(lane < edge + HMAX, after, 0.0))


def sides(core_ref, near, far):
    near, far = near.astype(F32), far.astype(F32)
    first = core_ref[0] == 0
    return jnp.where(first, far, near), jnp.where(first, near, far)


def rows_kernel(core_ref, even_ref, field_ref, near_ref, far_ref, one_ref, two_ref):
    rows = field_ref.shape[0]
    ends = []
    for r in (0, rows - 1):
        left, right = sides(core_ref, near_ref[r // 6], far_ref[r // 6])
        ends.append(jnp.concatenate(widened(field_ref[r], left, right, r % 6), axis=1))
    even = even_ref[0] == 1
    one_ref[0] = jnp.where(even, ends[1], ends[0]).astype(BF16)
    two_ref[0] = jnp.where(even, ends[0], ends[1]).astype(BF16)


def toeplitz_kernel(
    spans, core_ref, even_ref, field_ref, near_ref, far_ref, one_ref, two_ref, base_ref, weight_ref,
    out_ref, ext_ref, rest_ref, band_ref,
):
    rows, channels, cols = field_ref.shape
    lane = lax.broadcasted_iota(jnp.int32, (channels, LANES), 1)
    wanted = [i for first, last in spans for i in range(first, last)]
    for r in range(rows + 2):
        if not any(i in wanted for i in (r - 2, r - 1, r)):
            continue
        if r in (0, rows + 1):
            a, b = (one_ref, two_ref) if r else (two_ref, one_ref)
            row = jnp.where(even_ref[0] == 1, a[0].astype(F32), b[0].astype(F32))
            one, two = row[:, :LANES], row[:, LANES:]
        else:
            g, m = divmod(r - 1, 6)
            left, right = sides(core_ref, near_ref[g], far_ref[g])
            one, two = widened(field_ref[r - 1], left, right, m)
        ext_ref[r, :, :LANES] = one.astype(BF16)
        ext_ref[r, :, LANES:] = two.astype(BF16)
        for a in range(3):
            i = r - a
            if i in wanted:
                part = pltpu.roll(two, 2 * HMAX * a, 1) if a else two
                inside = (lane >= 2 * HMAX * a) & (lane < 2 * HMAX * (a + 1))
                rest_ref[i] = jnp.where(inside, part, rest_ref[i] if a else 0.0)

    r = lax.broadcasted_iota(jnp.int32, (LANES, LANES), 0)
    s = lax.broadcasted_iota(jnp.int32, (LANES, LANES), 1)

    def one_row(row, at):
        for k in range(BASES):
            cols_k = slice(k * LANES, (k + 1) * LANES)
            spill = []
            for a in range(3):
                line = base_ref[row, k * 3 + a : k * 3 + a + 1, :]
                circ = pltpu.roll(
                    jnp.broadcast_to(line, (LANES, LANES)), 0, 1, stride=1, stride_axis=0
                )
                band_ref[a * LANES : (a + 1) * LANES, cols_k] = jnp.where(s <= r, circ, 0.0).astype(
                    BF16
                )
                spill.append(jnp.where(s > r, circ, 0.0)[: 2 * HMAX])
            spill.append(jnp.zeros((LANES - 6 * HMAX, LANES), F32))
            band_ref[3 * LANES :, cols_k] = jnp.concatenate(spill, axis=0).astype(BF16)
        lines = [ext_ref[row + a] for a in range(3)]
        upper = [v[:, :LANES] for v in lines] + [rest_ref[row].astype(BF16)]
        lower = [v[:, LANES:] for v in lines] + [jnp.zeros((channels, LANES), BF16)]
        lhs = jnp.concatenate(
            [jnp.concatenate(upper, axis=1), jnp.concatenate(lower, axis=1)], axis=0
        )
        sums = jnp.dot(lhs, band_ref[...], preferred_element_type=F32).astype(BF16)
        stacked = jnp.concatenate(
            [
                jnp.concatenate(
                    [
                        sums[u * channels : (u + 1) * channels, k * LANES : (k + 1) * LANES]
                        for u in range(2)
                    ],
                    axis=1,
                )
                for k in range(BASES)
            ],
            axis=0,
        )
        mixed = jnp.dot(weight_ref[...], stacked, preferred_element_type=F32)
        out_ref[at] = mixed[:, :cols]

    done = 0
    for first, last in spans:
        pl.loop(first, last)(lambda row, shift=done - first: one_row(row, row + shift))
        done += last - first


def early_kernel(core_ref, field_ref, near_ref, far_ref, base_ref, weight_ref, *refs):
    toeplitz_kernel(
        (EARLY,), core_ref, None, field_ref, near_ref, far_ref, None, None, base_ref, weight_ref, *refs
    )


def late_kernel(*refs):
    toeplitz_kernel(((0, EARLY[0]), (EARLY[1], 16)), *refs)


def lat_rows_of(field, scalars, near, far):
    row = struct(BF16, 1, field.shape[1], 2 * LANES)
    one, two = call(
        rows_kernel, (row, row), *scalars, field, near, far, smem=2, flops=2 * 10**10
    )
    lat = ("zl", "x")
    one, two, far = lax.optimization_barrier((one, two, far))
    one = lax.ppermute(one, lat, [(i, i ^ 1) for i in range(32)])
    two = lax.ppermute(two, lat, [(i, i + 1 if i % 2 else i - 1) for i in range(1, 31)])
    return far, one, two


def taps_of(channels, disco_reach, disco_taps, disco_weight):
    lat_rows = disco_taps.shape[0]
    offsets = jnp.abs(jnp.arange(TAPS, dtype=jnp.int32) - HMAX)
    within = offsets[None, :] <= disco_reach[:, None]
    coef = jnp.where(
        within[:, None, :], disco_taps.reshape(lat_rows, BASES * 3, TAPS), 0.0
    )
    base = jnp.concatenate(
        [
            coef[:, :, :1],
            jnp.zeros((lat_rows, BASES * 3, LANES - TAPS), F32),
            coef[:, :, :0:-1],
        ],
        axis=2,
    )
    weight = disco_weight.transpose(2, 0, 1).reshape(channels, BASES * channels)
    return base, weight


def disco(kernel, count, field, scalars, around, base, weight):
    lat_rows, channels, lon_cols = field.shape
    return call(
        kernel,
        struct(F32, count, channels, lon_cols),
        *scalars,
        field,
        *around,
        base,
        weight,
        smem=len(scalars),
        flops=2 * count * 128 * 512 * 512,
        scratch=[
            pltpu.VMEM((lat_rows + 2, channels, 2 * LANES), BF16),
            pltpu.VMEM((lat_rows, channels, LANES), F32),
            pltpu.VMEM((4 * LANES, BASES * LANES), BF16),
        ],
    )


def exchange(cells, axes):
    return lax.all_to_all(cells, axes, split_axis=0, concat_axis=0, tiled=True)


def line_exchange(cells):
    groups = [
        [zl * 16 + member(pair, m) for m in range(2) for zl in range(8)] for pair in range(8)
    ]
    return lax.all_to_all(
        cells, ("zl", *LON), split_axis=0, concat_axis=0, tiled=True, axis_index_groups=groups
    )


def per_device(grid_field, disco_reach, disco_taps, disco_weight, legendre, mixing):
    lat_rows, lon_cols, channels = grid_field.shape
    wide = 2 * channels
    own = mixing.shape[0]
    place = lax.axis_index(LON)
    field = grid_field.transpose(0, 2, 1)
    forward = table(lon_cols, 1.0 / math.sqrt(NLON), lambda sector: np.arange(MODES))
    inverse = table(lon_cols, 1.0 / math.sqrt(MODES), lambda sector: orders_at(sector // 2 % 2))
    forward = lax.dynamic_index_in_dim(jnp.asarray(forward), place, 0, keepdims=False)
    inverse = lax.dynamic_index_in_dim(jnp.asarray(inverse), place, 0, keepdims=False)
    spread = [pltpu.VMEM((MODES * lat_rows, wide), F32)]

    core = lax.axis_index("core").reshape(1)
    even = (1 - lax.axis_index("x") % 2).reshape(1)
    waves = call(
        forward_kernel, struct(BF16, 16, 2 * lat_rows, wide), field, forward, scratch=spread
    )
    waves = exchange(waves, LON)
    packed = struct(BF16, 3, channels, LANES)
    near, far = call(edges_kernel, (packed, packed), core, field, smem=1)
    near = lax.ppermute(near, LON, [(i, i ^ 1) for i in range(16)])
    base, taps_weight = taps_of(channels, disco_reach, disco_taps, disco_weight)
    weight = jnp.concatenate([mixing[:, 0], mixing[:, 1]], axis=2)
    legs = call(
        legs_kernel,
        struct(BF16, 4, 2 * lat_rows, 256),
        (place * 2).astype(jnp.int32).reshape(1),
        legendre,
        jnp.asarray(degree_order()),
        smem=1,
        scratch=[
            pltpu.VMEM((2 * lat_rows, 768), F32),
            pltpu.VMEM((2, 8 * lat_rows, LANES), F32),
        ],
    )
    waves, near, far, legs, inverse, base, taps_weight, weight = lax.optimization_barrier(
        (waves, near, far, legs, inverse, base, taps_weight, weight)
    )
    message = call(spectra_kernel, struct(BF16, 4, 2 * lat_rows, 384), waves, legs)
    message = exchange(message, ("x",))
    coeffs, leg, mine = call(
        analysis_kernel,
        (
            struct(BF16, 8, 2 * own, wide),
            struct(BF16, 2, 4 * lat_rows, 256),
            struct(BF16, 6, 4 * lat_rows, LANES),
        ),
        message,
        far,
    )
    coeffs = exchange(coeffs, ("zl",))
    swap = [(i, member(pair_of(i), i % 2)) for i in range(16)]
    far = lax.ppermute(mine, LON, swap)
    far, one, two = lat_rows_of(field, (core, even), near, far)
    mixed = call(mixing_kernel, struct(BF16, 16, 2 * own, wide), coeffs, weight)
    mixed = line_exchange(mixed)
    early = disco(
        early_kernel, EARLY[1] - EARLY[0], field, (core,), (near, far), base, taps_weight
    )
    mixed, one, two, early = lax.optimization_barrier((mixed, one, two, early))
    modes = call(
        synthesis_kernel,
        struct(BF16, 32, 4 * lat_rows, wide),
        1 - core,
        mixed,
        leg,
        far,
        smem=1,
    )
    modes = exchange(modes, ("x", "y", "core"))
    late = disco(
        late_kernel,
        lat_rows - EARLY[1] + EARLY[0],
        field,
        (core, even),
        (near, far, one, two),
        base,
        taps_weight,
    )
    out = call(
        final_kernel,
        struct(BF16, lat_rows, channels, lon_cols),
        modes,
        inverse,
        early,
        late,
        field,
        scratch=spread,
    )
    return out.transpose(0, 2, 1)


def solution(mesh):
    fine = Mesh(mesh.devices.reshape(8, 4, 4, 2, 2), ("zl", "x", "y", "zh", "core"))
    lat, lon = ("zl", "x"), LON
    in_specs = (
        P(lat, lon, None),
        P(lat),
        P(lat, None),
        P(),
        P(lat, lon, None),
        P(lat, None, None, None),
    )
    return jax.shard_map(
        per_device, mesh=fine, in_specs=in_specs, out_specs=P(lat, lon, None), check_vma=False
    )
```
